128 devices in a mesh: pool: 2 (over y_hi), dom: 32 (over x, z, core), band: 2 (over y_lo).
Axes of the slice: x: 4, y: 4 (y_hi: 2, y_lo: 2; y = y_hi * 2 + y_lo), z: 4, core: 2. Of those that a mesh axis runs over, the one named last changes fastest.
Arguments:
- states_in: float32 [2, 32, 128, 19200], P('pool', 'dom', 'band'), may hold values from -6 to 6
- bloch_flip: int32 [2, 3], P('pool'), may hold values from 0 to 1
- kweight_num: int32 [2], P('pool'), may hold values from 1 to 7
- local_pot: float32 [32, 19200], P('dom'), may hold values from -1 to 1
- proj_values: float32 [32, 64, 19200], P('dom'), may hold values from -0.046875 to 0.046875
- proj_ids: int32 [32, 64], P('dom'), may hold values from 0 to 511, all different within a row
- coupling: float32 [512], replicated, may hold values from 0.5 to 2
- occupation: float32 [128], P('band'), may hold values from 0.5 to 2
Outputs:
- filtered: float32 [2, 32, 128, 19200], P('pool', 'dom', 'band')
- density: float32 [32, 19200], P('dom', ('pool', 'band'))
The draws below stay inside these ranges and needn't reach their ends.
Inputs may be any that keep to these rules, and one draw needn't show every extreme that they name: `proj_ids`: each box names 64 different projectors, and every projector is named by some box.
All inputs are finite; a program needn't handle non-finite values.
Results may differ from the reference program's by a relative error of at most 0.0001.
Values sent between devices are 32-bit elements; how exact they have to be, the bound alone decides.
A program may use at most 256 MiB of HBM per device.

```python
import math
import jax
import jax.numpy as jnp
import numpy as np
from jax import lax

STATES = 128
PROJ_BOX = 16
SLOTS = 64
HALO = 6
CX = 24
CY = 20
CZ = 40
NPROJ = 512
N_POOL = 2
N_DOM = 32


def touch_ends(entries, key, least, top_value):
    spot = [jax.random.randint(jax.random.fold_in(key, axis), (), 0, length) for axis, length in enumerate(entries.shape)]
    longest = entries.shape.index(max(entries.shape))
    beside = spot[:longest] + [(spot[longest] + 1) % entries.shape[longest]] + spot[longest + 1:]
    return entries.at[tuple(spot)].set(least).at[tuple(beside)].set(top_value)


def levels(rng, shape, split, low, largest):
    factor_of, own = 1.0, jax.random.fold_in(rng, 6)
    for axis_at, blocks in split:
        draws = jnp.exp(jax.random.uniform(jax.random.fold_in(own, axis_at), (blocks,), jnp.float32, low / len(split), largest / len(split)))
        factor_of = factor_of * jnp.repeat(draws, shape[axis_at] // blocks).reshape([-1 if axis == axis_at else 1 for axis in range(len(shape))])
    return factor_of


def picks_of(stream_key, rows, number_of, top, lift):
    sequence = jax.random.permutation(jax.random.fold_in(stream_key, 1), number_of)
    pull = sequence
    for power in range(3):
        pull = pull * pull // number_of
    pull = pull * lift // number_of
    tickets = jax.random.randint(jax.random.fold_in(stream_key, 2), (rows, number_of), 0, 4096) + pull
    sure = jax.random.permutation(jax.random.fold_in(stream_key, 3), rows)[jnp.arange(number_of) % rows]
    tickets = jnp.where(jnp.arange(rows)[:, None] == sure[None, :], 1 << 14, tickets)
    score = tickets * number_of + jnp.arange(number_of)
    return lax.top_k(score.astype(jnp.int32), top)[1].astype(jnp.int32)


def scatter_about(stream_key, shape, spread, bound, shards=(), held_as=jnp.bfloat16):
    result = spread * jax.random.normal(stream_key, shape, jnp.float32)
    if shards:
        result = result * levels(stream_key, shape, shards, -0.22, 0.18)
    return jnp.clip(result, -bound, bound).astype(held_as)


def setup_inputs(seed: int = 0) -> dict:
    streams_of = jax.random.split(jax.random.key(seed), 9)
    return {
        "states_in": scatter_about(streams_of[0], (N_POOL, N_DOM, STATES, CX * CY * CZ), 1.0, 6.0, ((0, 2), (1, 32), (2, 2)), jnp.float32),
        "bloch_flip": touch_ends(jax.random.randint(streams_of[1], (N_POOL, 3), 0, 2), jax.random.fold_in(streams_of[1], 1), 0, 1).astype(jnp.int32),
        "kweight_num": jax.random.randint(streams_of[2], (N_POOL,), 1, 8).astype(jnp.int32),
        "local_pot": jnp.clip(jax.random.uniform(streams_of[3], (N_DOM, CX * CY * CZ), jnp.float32, -1.0, 1.0) * levels(streams_of[3], (N_DOM, CX * CY * CZ), ((0, 32),), -0.4, 0.0), -1.0, 1.0),
        "proj_values": scatter_about(streams_of[4], (N_DOM, SLOTS, CX * CY * CZ), (CX * CY * CZ * SLOTS // (4 * PROJ_BOX)) ** -0.5, 0.046875, ((0, 32),), jnp.float32),
        "proj_ids": picks_of(streams_of[5], N_DOM, NPROJ, SLOTS, 0),
        "coupling": jnp.clip(jnp.exp(jax.random.uniform(streams_of[6], (NPROJ,), jnp.float32, math.log(0.5), math.log(2.0))), 0.5, 2.0),
        "occupation": jnp.clip(jnp.exp(math.log(2.0) - 1.3862944 * jax.random.uniform(streams_of[7], (STATES,), jnp.float32) ** levels(streams_of[7], (STATES,), ((0, 2),), -0.2, 0.2)), 0.5, 2.0),
    }


COEFFS = (-5369.0 / 1800.0, 12.0 / 7.0, -15.0 / 56.0, 10.0 / 189.0, -1.0 / 112.0, 2.0 / 1925.0, -1.0 / 16632.0)
CENTER = 14.0
HALF_WIDTH = 10.0


def gray_order(count):
    return np.array([c ^ (c >> 1) for c in range(count)], dtype=np.int32)


def to_grid(boxes):
    box_y = min(4, N_DOM // 4)
    box_x = N_DOM // (2 * box_y)
    shaped = boxes.reshape(box_x, box_y, 2, STATES, CX, CY, CZ)
    shaped = shaped[gray_order(box_x)][:, gray_order(box_y)]
    shaped = jnp.transpose(shaped, (3, 0, 4, 1, 5, 2, 6))
    return shaped.reshape(STATES, box_x * CX, box_y * CY, 2 * CZ)


def from_grid(grid):
    box_y = min(4, N_DOM // 4)
    box_x = N_DOM // (2 * box_y)
    shaped = grid.reshape(STATES, box_x, CX, box_y, CY, 2, CZ)
    shaped = jnp.transpose(shaped, (1, 3, 5, 0, 2, 4, 6))
    shaped = shaped[gray_order(box_x)][:, gray_order(box_y)]
    return shaped.reshape(N_DOM, STATES, CX, CY, CZ)


def second_diff(grid, axis, sign):
    width = grid.shape[axis]
    ext = jnp.concatenate([sign * lax.slice_in_dim(grid, width - HALO, width, axis=axis), grid,
                           sign * lax.slice_in_dim(grid, 0, HALO, axis=axis)], axis=axis)
    acc = COEFFS[0] * grid
    for shift in range(1, HALO + 1):
        acc = acc + COEFFS[shift] * (lax.slice_in_dim(ext, HALO + shift, HALO + shift + width, axis=axis)
                                     + lax.slice_in_dim(ext, HALO - shift, HALO - shift + width, axis=axis))
    return acc


def hamilton(boxes, signs, local_pot, proj_flat, onehot, coupling):
    grid = to_grid(boxes)
    lap = second_diff(grid, 1, signs[0]) + second_diff(grid, 2, signs[1]) + second_diff(grid, 3, signs[2])
    kinetic = from_grid(-0.5 * lap)
    flat = boxes.reshape(N_DOM, STATES, CX * CY * CZ)
    hi = lax.Precision.HIGHEST
    coef = jnp.einsum('bsc,bjc->bsj', flat, proj_flat, precision=hi)
    total = jnp.einsum('bsj,bjp->sp', coef, onehot, precision=hi)
    scaled = total * coupling[None, :]
    back = jnp.einsum('sp,bjp->bsj', scaled, onehot, precision=hi)
    nonlocal_part = jnp.einsum('bsj,bjc->bsc', back, proj_flat, precision=hi).reshape(boxes.shape)
    return kinetic + local_pot[:, None] * boxes + nonlocal_part


def reference(states_in, bloch_flip, kweight_num, local_pot, proj_values, proj_ids, coupling, occupation):
    states_box = states_in.reshape(N_POOL, N_DOM, STATES, CX, CY, CZ)
    potential = local_pot.reshape(N_DOM, CX, CY, CZ)
    proj_flat = proj_values
    onehot = (proj_ids[:, :, None] == jnp.arange(NPROJ, dtype=jnp.int32)[None, None, :]).astype(jnp.float32)
    numer = kweight_num.astype(jnp.float32)
    total_num = jnp.sum(numer)
    outs = []
    density = jnp.zeros((N_DOM, CX, CY, CZ), jnp.float32)
    for point in range(N_POOL):
        signs = 1.0 - 2.0 * bloch_flip[point].astype(jnp.float32)
        start = states_box[point]
        first = (hamilton(start, signs, potential, proj_flat, onehot, coupling) - CENTER * start) / HALF_WIDTH
        second = 2.0 * (hamilton(first, signs, potential, proj_flat, onehot, coupling) - CENTER * first) / HALF_WIDTH - start
        outs.append(second)
        own = jnp.sum(occupation[None, :, None, None, None] * second * second, axis=1)
        density = density + numer[point] * own
    filtered = jnp.stack(outs, axis=0).reshape(N_POOL, N_DOM, STATES, CX * CY * CZ)
    return filtered, (density / total_num).reshape(N_DOM, CX * CY * CZ)
```

```python
import jax
import jax.numpy as jnp
import numpy as np
from jax import lax
from jax.experimental import pallas as pl
from jax.experimental.pallas import tpu as pltpu
from jax.sharding import PartitionSpec as P

MESH = pl.DeviceIdType.MESH
F32 = jnp.float32
BF16 = jnp.bfloat16

HALO = 6
CX = 24
CY = 20
CZ = 40
CELLS = CX * CY * CZ
COEFFS = (
    -5369.0 / 1800.0,
    12.0 / 7.0,
    -15.0 / 56.0,
    10.0 / 189.0,
    -1.0 / 112.0,
    2.0 / 1925.0,
    -1.0 / 16632.0,
)
CENTER = 14.0
HALF_WIDTH = 10.0
SCALE = -0.5 / HALF_WIDTH

GROUPS = 3
XL = CX // GROUPS
ROWS = XL * CY
USED = GROUPS * CZ
THIRD = CELLS // GROUPS
BLOCKS = 10
LINES = 16
STATES = 64
CH = 8
SLOTS = 64
PAIRS = ROWS // 2
YROWS = 45
XROWS = 40
PIECE = 4864
NOTE = PIECE + 128

Y_MASKS = (2, 4, 6)
X_MASKS = (8, 16, 24)
ALL_MASKS = (1,) + Y_MASKS + X_MASKS


def z_matrices():
    own = np.zeros((128, 128), np.float64)
    low = np.zeros((128, 128), np.float64)
    up = np.zeros((128, 128), np.float64)
    for group in range(GROUPS):
        for z in range(CZ):
            for shift in range(1, HALO + 1):
                for source in (z + shift, z - shift):
                    target = own if 0 <= source < CZ else (low if source < 0 else up)
                    target[group * CZ + source % CZ, group * CZ + z] += SCALE * COEFFS[shift]
    pairs = []
    for matrix in (own, low, up):
        high = jnp.asarray(matrix, F32).astype(BF16)
        rest = (jnp.asarray(matrix, F32) - high.astype(F32)).astype(BF16)
        pairs.append(jnp.concatenate([high, rest], axis=1))
    return pairs


def flip_bits(me, mask):
    other = me
    for bit in (1, 2, 4, 8, 16):
        if mask & bit:
            other = other + bit * (1 - 2 * ((me // bit) % 2))
    return other


def lanes_of(rows):
    return lax.broadcasted_iota(jnp.int32, (rows, 128), 1)


def roll(value, shift):
    shift = shift % 128
    if shift == 0:
        return value
    return pltpu.roll(value, shift, value.ndim - 1)


def split(value):
    high = value.astype(BF16)
    return high, (value - high.astype(F32)).astype(BF16)


def rows_from_lines(load, count, put):
    lane = lanes_of(count)
    tiles = [[load(group, tile) for tile in range(5)] for group in range(GROUPS)]
    for line in range(LINES):
        tile, offset = divmod(CZ * line, 128)
        parts = []
        for group in range(GROUPS):
            value = tiles[group][tile]
            if offset + CZ > 128:
                value = jnp.where(lane >= offset, value, tiles[group][tile + 1])
            parts.append(roll(value, CZ * group - offset))
        row = jnp.where(lane < CZ, parts[0], jnp.where(lane < 2 * CZ, parts[1], parts[2]))
        put(line, jnp.where(lane < USED, row, 0.0))


def lines_from_rows(rows, put):
    lane = lanes_of(8)
    for group in range(GROUPS):
        for tile in range(5):
            first, offset = divmod(128 * tile, CZ)
            value = None
            for step in range(4):
                part = roll(rows[first + step], CZ * step - offset - CZ * group)
                value = part if step == 0 else jnp.where(lane < CZ * step - offset, value, part)
            put(group, tile, value)


def kernel(
    states,
    flips,
    numer,
    pot,
    proj,
    ids,
    coupling,
    occupation,
    k_own,
    k_low,
    k_up,
    out,
    dens,
    cur,
    nxt,
    nonloc,
    pbox,
    send_y,
    send_x,
    recv_y,
    recv_x,
    recv_z,
    ext_x,
    ext_y,
    potential,
    kz,
    gather1,
    gather2,
    same,
    occ_rows,
    square,
    rho,
    notes,
    got_notes,
    stage_in,
    stage_out,
    in_sem,
    out_sem,
    send_sem,
    recv_sem,
    gsend_sem,
    grecv_sem,
    nsend_sem,
    nrecv_sem,
):
    me = lax.axis_index("dom")
    pool = lax.axis_index("pool")
    band = lax.axis_index("band")
    core = me % 2
    code_y = (me // 2) % 4
    code_x = me // 8

    def place_of(code):
        return code + (code // 2) * (1 - 2 * (code % 2))

    place_y = place_of(code_y)
    place_x = place_of(code_x)
    odd_y = place_y % 2
    odd_x = place_x % 2

    def in_copy(job):
        source = states if job < 4 else proj
        return pltpu.make_async_copy(
            source.at[pl.ds(16 * (job % 4), 16)], stage_in.at[job % 3], in_sem.at[job % 3]
        )

    for job in range(3):
        in_copy(job).start()

    barrier = pltpu.get_barrier_semaphore()
    for mask in ALL_MASKS:
        pl.semaphore_signal(
            barrier, inc=1, device_id={"dom": flip_bits(me, mask)}, device_id_type=MESH
        )
    mates = []
    for relation in range(1, 4):
        mate_pool = (pool + relation // 2) % 2
        mate_band = (band + relation % 2) % 2
        mates.append((mate_pool, mate_band))
        pl.semaphore_signal(
            barrier,
            inc=1,
            device_id={"pool": mate_pool, "band": mate_band},
            device_id_type=MESH,
        )

    def sign_of(direction, at_edge):
        sign = 1.0 - 2.0 * flips[0, direction].astype(F32)
        return jnp.where(at_edge, sign, jnp.float32(1.0))

    low_x, up_x = sign_of(0, place_x == 0), sign_of(0, place_x == 3)
    low_y, up_y = sign_of(1, place_y == 0), sign_of(1, place_y == 3)
    low_z, up_z = sign_of(2, core == 0), sign_of(2, core == 1)

    def halo_copies(phase, chunk):
        turn = CH * phase + chunk
        source = cur if phase == 0 else nxt
        plan = (
            (send_y.at[chunk, 1 - odd_y], recv_y.at[turn, 0], 2),
            (send_y.at[chunk, odd_y], recv_y.at[turn, 1], 4),
            (send_x.at[chunk, 1 - odd_x], recv_x.at[turn, 0], 8),
            (send_x.at[chunk, odd_x], recv_x.at[turn, 1], 16),
            (source.at[chunk], recv_z.at[turn], 1),
        )
        return [
            pltpu.make_async_remote_copy(
                src_ref=src,
                dst_ref=dst,
                send_sem=send_sem.at[turn, at],
                recv_sem=recv_sem.at[turn, at],
                device_id={"dom": flip_bits(me, mask)},
                device_id_type=MESH,
            )
            for at, (src, dst, mask) in enumerate(plan)
        ]

    lane8 = lax.broadcasted_iota(jnp.int32, (1, 8, 128), 2)

    def enqueue(phase, chunk):
        source = cur if phase == 0 else nxt
        copies = halo_copies(phase, chunk)
        copies[4].start()
        for face, first in ((0, 0), (1, CY - HALO)):
            value = jnp.concatenate(
                [source[chunk, pl.ds(x * CY + first, HALO)] for x in range(XL)], axis=0
            )
            tail = value[YROWS : YROWS + 3]
            for piece in range(15):
                send_y[chunk, face, 3 * piece : 3 * piece + 3] = jnp.where(
                    lane8 < USED, value[3 * piece : 3 * piece + 3], roll(tail, USED - 8 * piece)
                )
        copies[0].start()
        copies[1].start()
        for face, first in ((0, 0), (1, 2 * CY)):
            parts = [
                roll(
                    source[chunk, pl.ds(first + XROWS * group, XROWS)],
                    CZ * group - (GROUPS - 1) * CZ * face,
                )
                for group in range(GROUPS)
            ]
            send_x[chunk, face] = jnp.where(
                lane8 < CZ, parts[0], jnp.where(lane8 < 2 * CZ, parts[1], parts[2])
            )
        copies[2].start()
        copies[3].start()

    def stencil(phase, chunk):
        turn = CH * phase + chunk
        source, target = (cur, nxt) if phase == 0 else (nxt, cur)

        def z_part(half, carry):
            at = pl.ds(half * (ROWS // 2), ROWS // 2)
            left = jnp.concatenate(
                [
                    source[chunk, at].reshape(ROWS * 4, 128),
                    recv_z[turn, at].reshape(ROWS * 4, 128),
                ],
                axis=1,
            )
            high, rest = split(left)
            wide = jnp.dot(high, kz[...], preferred_element_type=F32)
            narrow = jnp.dot(rest, kz[:, :128], preferred_element_type=F32)
            total = (wide[:, :128] + wide[:, 128:] + narrow).reshape(ROWS // 2, 8, 128)
            if phase == 0:
                target[chunk, at] = total
            else:
                target[chunk, at] = total + total - target[chunk, at]
            return carry

        lax.fori_loop(0, 2, z_part, 0)

        for slot_of, sign, first in ((1 - odd_y, low_y, 0), (odd_y, up_y, HALO + CY)):
            rows = []
            tail = jnp.zeros((3, 8, 128), F32)
            for piece in range(15):
                value = recv_y[turn, slot_of, 3 * piece : 3 * piece + 3]
                rows.append(value)
                moved = roll(value, 8 * piece - USED)
                tail = jnp.where((lane8 >= 8 * piece) & (lane8 < 8 * piece + 8), moved, tail)
            rows = jnp.concatenate(rows + [tail], axis=0)
            rows = jnp.where(lane8 < USED, rows * sign, 0.0)
            for x in range(XL):
                ext_y[x, first : first + HALO] = rows[HALO * x : HALO * x + HALO]
        for x in range(XL):
            ext_y[x, HALO : HALO + CY] = source[chunk, x * CY : x * CY + CY]

        for group in range(GROUPS):
            lower = recv_x[turn, 1 - odd_x] * low_x
            ext_x[XROWS * group : XROWS * group + XROWS] = jnp.where(
                lane8 < CZ,
                roll(lower, -CZ * group),
                roll(source[chunk, pl.ds(2 * CY + XROWS * group, XROWS)], CZ),
            )
            upper = recv_x[turn, odd_x] * up_x
            start = (HALO + XL) * CY + XROWS * group
            ext_x[start : start + XROWS] = jnp.where(
                lane8 >= 2 * CZ,
                roll(upper, CZ * (GROUPS - 1 - group)),
                roll(source[chunk, pl.ds(XROWS * group, XROWS)], -CZ),
            )
        ext_x[HALO * CY : (HALO + XL) * CY] = source[chunk]

        def rest_part(step, carry):
            x, half = step // 2, step % 2
            at = pl.ds(x * CY + half * 10, 10)
            column = ext_y[x, pl.ds(half * 10, 10 + 2 * HALO)]
            total = potential[at] * column[HALO : HALO + 10]
            for shift in range(1, HALO + 1):
                pair = column[HALO + shift : HALO + shift + 10] + column[HALO - shift : HALO - shift + 10]
                above = ext_x[pl.ds((x + HALO + shift) * CY + half * 10, 10)]
                below = ext_x[pl.ds((x + HALO - shift) * CY + half * 10, 10)]
                total = total + (SCALE * COEFFS[shift]) * (pair + (above + below))
            if phase == 0:
                target[chunk, at] = target[chunk, at] + total
            else:
                target[chunk, at] = target[chunk, at] + (total + total)
            return carry

        lax.fori_loop(0, 2 * XL, rest_part, 0)

    own_slot = core * 16 + me // 2

    def gather_copies(phase, stage):
        buffer = gather1 if phase == 0 else gather2
        if stage == 0:
            masks, block = Y_MASKS, buffer.at[own_slot]
        elif stage == 1:
            masks, block = X_MASKS, buffer.at[pl.ds(core * 16 + code_x * 4, 4)]
        else:
            masks, block = (1,), buffer.at[pl.ds(core * 16, 16)]
        return [
            pltpu.make_async_remote_copy(
                src_ref=block,
                dst_ref=block,
                send_sem=gsend_sem.at[phase, 3 * stage + at],
                recv_sem=grecv_sem.at[phase, 3 * stage + at],
                device_id={"dom": flip_bits(me, mask)},
                device_id_type=MESH,
            )
            for at, mask in enumerate(masks)
        ]

    def gather_start(phase, stage):
        for copy in gather_copies(phase, stage):
            copy.start()

    def gather_wait(phase, stage):
        for copy in gather_copies(phase, stage):
            copy.wait()

    lane32 = lanes_of(32)

    def coefficients(phase):
        source = cur if phase == 0 else nxt
        buffer = gather1 if phase == 0 else gather2

        def step(pair, total):
            left = jnp.concatenate(
                [source[:, 2 * pair + part].reshape(STATES, 128) for part in range(2)], axis=1
            )
            both = jnp.concatenate(split(left), axis=0)
            return total + lax.dot_general(
                both, pbox[pair], (((1,), (1,)), ((), ())), preferred_element_type=F32
            )

        total = lax.fori_loop(0, PAIRS, step, jnp.zeros((128, 128), F32), unroll=4)
        total = total + roll(total, 64)
        total = total[:STATES] + total[STATES:]
        buffer[own_slot, 0:32] = jnp.where(lane32 < 64, total[:32], total[32:])

    def nonlocal_rows(phase):
        buffer = gather1 if phase == 0 else gather2

        def step(slot, total):
            block = buffer[slot, 0:32]
            pieces = []
            for piece in split(block):
                wide = piece.astype(F32)
                pieces.append(jnp.where(lane32 < 64, wide, 0.0))
                pieces.append(jnp.where(lane32 < 64, 0.0, wide))
            left = jnp.concatenate(pieces, axis=0).astype(BF16)
            return total + lax.dot_general(
                left, same[slot], (((1,), (1,)), ((), ())), preferred_element_type=F32
            )

        total = lax.fori_loop(0, 32, step, jnp.zeros((128, 128), F32), unroll=4)
        weights = (total[:STATES] + total[STATES:]) * coupling_row
        weights = weights * ((phase + 1.0) / HALF_WIDTH)
        left = jnp.concatenate(split(weights), axis=1)

        def spread(pair, carry):
            right = jnp.concatenate([pbox[pair], pbox[pair]], axis=0)
            both = jnp.dot(left, right, preferred_element_type=F32)
            nonloc[:, 2 * pair] = both[:, :128].reshape(CH, 8, 128)
            nonloc[:, 2 * pair + 1] = both[:, 128:].reshape(CH, 8, 128)
            return carry

        lax.fori_loop(0, PAIRS, spread, 0, unroll=4)

    def bring_states(job):
        in_copy(job).wait()

        def block(index, carry):
            for half in range(2):

                def load(group, tile):
                    start = pl.multiple_of(THIRD * group + 640 * index + 128 * tile, 128)
                    return stage_in[job % 3, 8 * half : 8 * half + 8, pl.ds(start, 128)]

                def put(line, row):
                    cur[2 * job + half, LINES * index + line] = row

                rows_from_lines(load, 8, put)
            return carry

        lax.fori_loop(0, BLOCKS, block, 0)
        in_copy(job + 3).start()

    bring_states(0)
    pl.semaphore_wait(barrier, len(ALL_MASKS) + 3)
    enqueue(0, 0)
    enqueue(0, 1)
    bring_states(1)
    enqueue(0, 2)
    bring_states(2)
    bring_states(3)

    kz[0:128] = k_own[...]
    kz[128:256] = (k_low[...].astype(F32) * low_z + k_up[...].astype(F32) * up_z).astype(BF16)

    def potential_block(index, carry):
        def load(group, tile):
            start = pl.multiple_of(THIRD * group + 640 * index + 128 * tile, 128)
            return jnp.broadcast_to(pot[:, pl.ds(start, 128)], (8, 128))

        def put(line, row):
            potential[LINES * index + line] = (row - CENTER) / HALF_WIDTH + 3.0 * SCALE * COEFFS[0]

        rows_from_lines(load, 8, put)
        return carry

    lax.fori_loop(0, BLOCKS, potential_block, 0)

    def diagonal(size):
        return lax.broadcasted_iota(jnp.int32, (size, size), 0) == lax.broadcasted_iota(
            jnp.int32, (size, size), 1
        )

    id_row = ids[...].astype(F32)
    id_pair = jnp.concatenate([id_row, id_row], axis=1)
    id_column = jnp.sum(jnp.where(diagonal(128), id_pair, 0.0), axis=1, keepdims=True)
    all_ids = lax.broadcasted_iota(jnp.int32, (128, 512), 1).astype(F32)
    strength = jnp.sum(
        jnp.where(all_ids == id_column, coupling[...], 0.0), axis=1, keepdims=True
    )
    coupling_row = jnp.sum(jnp.where(diagonal(128), strength, 0.0), axis=0, keepdims=True)
    occ_column = jnp.sum(
        jnp.where(diagonal(STATES), occupation[...], 0.0), axis=1, keepdims=True
    )
    occ_rows[...] = jnp.broadcast_to(occ_column, (STATES, 128)).reshape(CH, 8, 128)
    square[...] = jnp.zeros((ROWS, 8, 128), F32)
    gather1[own_slot, 32:40] = jnp.broadcast_to(id_pair, (8, 128))

    for job in range(4, 8):
        in_copy(job).wait()

        def proj_block(index, carry):
            held = []

            def load(group, tile):
                start = pl.multiple_of(THIRD * group + 640 * index + 128 * tile, 128)
                return stage_in[job % 3, :, pl.ds(start, 128)]

            def put(line, row):
                held.append(row)
                if line % 2 == 1:
                    high, rest = split(jnp.concatenate(held[-2:], axis=1))
                    pair = (LINES // 2) * index + line // 2
                    pbox[pair, 16 * (job - 4) : 16 * (job - 4) + 16] = high
                    pbox[pair, 16 * job : 16 * job + 16] = rest

            rows_from_lines(load, 16, put)
            return carry

        lax.fori_loop(0, BLOCKS, proj_block, 0)
        if job + 3 < 8:
            in_copy(job + 3).start()

    coefficients(0)
    gather_start(0, 0)

    def phase_one(chunk, carry):
        for copy in halo_copies(0, chunk):
            copy.wait()

        @pl.when(chunk == 2)
        def _():
            gather_wait(0, 0)
            gather_start(0, 1)

        @pl.when(chunk == 3)
        def _():
            gather_wait(0, 1)
            gather_start(0, 2)

        @pl.when((chunk >= 1) & (chunk < 6))
        def _():
            enqueue(0, chunk + 2)

        @pl.when(chunk >= 6)
        def _():
            enqueue(1, chunk - 6)

        stencil(0, chunk)

        @pl.when(chunk == 4)
        def _():
            gather_wait(0, 2)

            def compare(slot, inner):
                same[slot] = jnp.where(id_column == gather1[slot, 32:33], 1.0, 0.0).astype(BF16)
                return inner

            lax.fori_loop(0, 32, compare, 0)
            nonlocal_rows(0)

        def finish(done, inner):
            nxt[done] = nxt[done] + nonloc[done]
            return inner

        low = jnp.where(chunk == 4, 0, chunk)
        high = jnp.where(chunk < 4, chunk, chunk + 1)
        lax.fori_loop(low, high, finish, 0)
        return carry

    lax.fori_loop(0, CH, phase_one, 0)

    coefficients(1)
    gather_start(1, 0)

    def out_copy(chunk):
        return pltpu.make_async_copy(
            stage_out.at[chunk % 2], out.at[pl.ds(8 * chunk, 8)], out_sem.at[chunk % 2]
        )

    def phase_two(chunk, carry):
        for copy in halo_copies(1, chunk):
            copy.wait()

        @pl.when(chunk == 1)
        def _():
            gather_wait(1, 0)
            gather_start(1, 1)

        @pl.when(chunk == 2)
        def _():
            gather_wait(1, 1)
            gather_start(1, 2)

        @pl.when(chunk < 6)
        def _():
            enqueue(1, chunk + 2)

        stencil(1, chunk)

        @pl.when(chunk == 3)
        def _():
            gather_wait(1, 2)
            nonlocal_rows(1)

        def finish(done, inner):
            @pl.when(done >= 2)
            def _():
                out_copy(done - 2).wait()

            weight = occ_rows[done]

            def block(index, deep):
                at = pl.ds(LINES * index, LINES)
                value = cur[done, at] + nonloc[done, at]
                square[at] = square[at] + value * value * weight

                def put(group, tile, found):
                    start = pl.multiple_of(THIRD * group + 640 * index + 128 * tile, 128)
                    stage_out[done % 2, :, pl.ds(start, 128)] = found

                lines_from_rows([value[line] for line in range(LINES)], put)
                return deep

            lax.fori_loop(0, BLOCKS, block, 0)
            out_copy(done).start()
            return inner

        low = jnp.where(chunk == 3, 0, chunk)
        high = jnp.where(chunk < 3, chunk, chunk + 1)
        lax.fori_loop(low, high, finish, 0)
        return carry

    lax.fori_loop(0, CH, phase_two, 0)

    own_numer = numer[0].astype(F32)

    def rho_block(index, carry):
        value = square[pl.ds(LINES * index, LINES)]

        def put(group, tile, found):
            start = pl.multiple_of(THIRD * group + 640 * index + 128 * tile, 128)
            rho[:, pl.ds(start, 128)] = jnp.sum(found, axis=0, keepdims=True) * own_numer

        lines_from_rows([value[line] for line in range(LINES)], put)
        return carry

    lax.fori_loop(0, BLOCKS, rho_block, 0)
    for quarter in range(4):
        start = 128 * (75 * quarter // 2)
        notes[quarter, :, 0:PIECE] = rho[:, start : start + PIECE]
        notes[quarter, :, PIECE:NOTE] = jnp.full((1, 128), own_numer, F32)
    note_copies = [
        pltpu.make_async_remote_copy(
            src_ref=notes.at[2 * mate_pool + mate_band],
            dst_ref=got_notes.at[at],
            send_sem=nsend_sem.at[at],
            recv_sem=nrecv_sem.at[at],
            device_id={"pool": mate_pool, "band": mate_band},
            device_id_type=MESH,
        )
        for at, (mate_pool, mate_band) in enumerate(mates)
    ]
    for copy in note_copies:
        copy.start()
    for copy in note_copies:
        copy.wait()
    total = notes[2 * pool + band] + got_notes[0] + got_notes[1] + got_notes[2]
    count = total[:, PIECE : PIECE + 1] * 0.5
    dens[...] = total[:, :PIECE] / count
    for chunk in range(CH - 2, CH):
        out_copy(chunk).wait()


def body(
    states_in, bloch_flip, kweight_num, local_pot, proj_values, proj_ids, coupling, occupation
):
    k_own, k_low, k_up = z_matrices()
    vmem = pl.BlockSpec(memory_space=pltpu.VMEM)
    smem = pl.BlockSpec(memory_space=pltpu.SMEM)
    hbm = pl.BlockSpec(memory_space=pl.ANY)
    dma = pltpu.SemaphoreType.DMA
    out, dens = pl.pallas_call(
        kernel,
        out_shape=(
            jax.ShapeDtypeStruct((STATES, CELLS), F32),
            jax.ShapeDtypeStruct((1, PIECE), F32),
        ),
        in_specs=[hbm, smem, smem, vmem, hbm, vmem, vmem, vmem, vmem, vmem, vmem],
        out_specs=(hbm, vmem),
        scratch_shapes=[
            pltpu.VMEM((CH, ROWS, 8, 128), F32),
            pltpu.VMEM((CH, ROWS, 8, 128), F32),
            pltpu.VMEM((CH, ROWS, 8, 128), F32),
            pltpu.VMEM((PAIRS, 2 * SLOTS, 256), BF16),
            pltpu.VMEM((CH, 2, YROWS, 8, 128), F32),
            pltpu.VMEM((CH, 2, XROWS, 8, 128), F32),
            pltpu.VMEM((2 * CH, 2, YROWS, 8, 128), F32),
            pltpu.VMEM((2 * CH, 2, XROWS, 8, 128), F32),
            pltpu.VMEM((2 * CH, ROWS, 8, 128), F32),
            pltpu.VMEM(((XL + 2 * HALO) * CY, 8, 128), F32),
            pltpu.VMEM((XL, CY + 2 * HALO, 8, 128), F32),
            pltpu.VMEM((ROWS, 8, 128), F32),
            pltpu.VMEM((256, 256), BF16),
            pltpu.VMEM((32, 40, 128), F32),
            pltpu.VMEM((32, 32, 128), F32),
            pltpu.VMEM((32, 128, 128), BF16),
            pltpu.VMEM((CH, 8, 128), F32),
            pltpu.VMEM((ROWS, 8, 128), F32),
            pltpu.VMEM((1, CELLS), F32),
            pltpu.VMEM((4, 1, NOTE), F32),
            pltpu.VMEM((3, 1, NOTE), F32),
            pltpu.VMEM((3, 16, CELLS), F32),
            pltpu.VMEM((2, 8, CELLS), F32),
            dma((3,)),
            dma((2,)),
            dma((2 * CH, 5)),
            dma((2 * CH, 5)),
            dma((2, 9)),
            dma((2, 9)),
            dma((3,)),
            dma((3,)),
        ],
        compiler_params=pltpu.CompilerParams(
            collective_id=0, has_side_effects=True, vmem_limit_bytes=62 << 20
        ),
    )(
        states_in[0, 0],
        bloch_flip,
        kweight_num,
        local_pot,
        proj_values[0],
        proj_ids,
        coupling[None],
        occupation[None],
        k_own,
        k_low,
        k_up,
    )
    offset = 64 * lax.axis_index("band")
    quarter = lax.dynamic_slice(dens, (0, offset), (1, CELLS // 4))
    return out[None, None], quarter


def solution(mesh):
    placed = (
        P("pool", "dom", "band", None),
        P("pool", None),
        P("pool"),
        P("dom", None),
        P("dom", None, None),
        P("dom", None),
        P(),
        P("band"),
    )
    return jax.shard_map(
        body,
        mesh=mesh,
        in_specs=placed,
        out_specs=(P("pool", "dom", "band", None), P("dom", ("pool", "band"))),
        check_vma=False,
    )
```

```python
import jax
import jax.numpy as jnp
import numpy as np
from jax import lax
from jax.experimental import pallas as pl
from jax.experimental.pallas import tpu as pltpu
from jax.sharding import PartitionSpec as P

MESH = pl.DeviceIdType.MESH
F32 = jnp.float32
BF16 = jnp.bfloat16

HALO = 6
CX = 24
CY = 20
CZ = 40
CELLS = CX * CY * CZ
COEFFS = (
    -5369.0 / 1800.0,
    12.0 / 7.0,
    -15.0 / 56.0,
    10.0 / 189.0,
    -1.0 / 112.0,
    2.0 / 1925.0,
    -1.0 / 16632.0,
)
CENTER = 14.0
HALF_WIDTH = 10.0
SCALE = -0.5 / HALF_WIDTH

GROUPS = 3
XL = CX // GROUPS
ROWS = XL * CY
USED = GROUPS * CZ
THIRD = CELLS // GROUPS
BLOCKS = 10
LINES = 16
STATES = 64
CH = 8
SLOTS = 64
PAIRS = ROWS // 2
YROWS = 45
XROWS = 40
PIECE = 4864
NOTE = PIECE + 128

Y_MASKS = (2, 4, 6)
X_MASKS = (8, 16, 24)
ALL_MASKS = (1,) + Y_MASKS + X_MASKS


def z_matrices():
    own = np.zeros((128, 128), np.float64)
    low = np.zeros((128, 128), np.float64)
    up = np.zeros((128, 128), np.float64)
    for group in range(GROUPS):
        for z in range(CZ):
            for shift in range(1, HALO + 1):
                for source in (z + shift, z - shift):
                    target = own if 0 <= source < CZ else (low if source < 0 else up)
                    target[group * CZ + source % CZ, group * CZ + z] += SCALE * COEFFS[shift]
    pairs = []
    for matrix in (own, low, up):
        high = jnp.asarray(matrix, F32).astype(BF16)
        rest = (jnp.asarray(matrix, F32) - high.astype(F32)).astype(BF16)
        pairs.append(jnp.concatenate([high, rest], axis=1))
    return pairs


def flip_bits(me, mask):
    other = me
    for bit in (1, 2, 4, 8, 16):
        if mask & bit:
            other = other + bit * (1 - 2 * ((me // bit) % 2))
    return other


def lanes_of(rows):
    return lax.broadcasted_iota(jnp.int32, (rows, 128), 1)


def roll(value, shift):
    shift = shift % 128
    if shift == 0:
        return value
    return pltpu.roll(value, shift, value.ndim - 1)


def split(value):
    high = value.astype(BF16)
    return high, (value - high.astype(F32)).astype(BF16)


def rows_from_lines(load, count, put):
    lane = lanes_of(count)
    tiles = [[load(group, tile) for tile in range(5)] for group in range(GROUPS)]
    for line in range(LINES):
        tile, offset = divmod(CZ * line, 128)
        parts = []
        for group in range(GROUPS):
            value = tiles[group][tile]
            if offset + CZ > 128:
                value = jnp.where(lane >= offset, value, tiles[group][tile + 1])
            parts.append(roll(value, CZ * group - offset))
        row = jnp.where(lane < CZ, parts[0], jnp.where(lane < 2 * CZ, parts[1], parts[2]))
        put(line, jnp.where(lane < USED, row, 0.0))


def lines_from_rows(rows, put):
    lane = lanes_of(8)
    for group in range(GROUPS):
        for tile in range(5):
            first, offset = divmod(128 * tile, CZ)
            value = None
            for step in range(4):
                part = roll(rows[first + step], CZ * step - offset - CZ * group)
                value = part if step == 0 else jnp.where(lane < CZ * step - offset, value, part)
            put(group, tile, value)


def kernel(
    states,
    flips,
    numer,
    pot,
    proj,
    ids,
    coupling,
    occupation,
    k_own,
    k_low,
    k_up,
    out,
    dens,
    cur,
    nxt,
    nonloc,
    pbox,
    send_y,
    send_x,
    recv_y,
    recv_x,
    recv_z,
    ext_x,
    ext_y,
    potential,
    kz,
    gather1,
    gather2,
    same,
    occ_rows,
    square,
    rho,
    notes,
    got_notes,
    stage_in,
    in_sem,
    send_sem,
    recv_sem,
    gsend_sem,
    grecv_sem,
    nsend_sem,
    nrecv_sem,
):
    me = lax.axis_index("dom")
    pool = lax.axis_index("pool")
    band = lax.axis_index("band")
    core = me % 2
    code_y = (me // 2) % 4
    code_x = me // 8

    def place_of(code):
        return code + (code // 2) * (1 - 2 * (code % 2))

    place_y = place_of(code_y)
    place_x = place_of(code_x)
    odd_y = place_y % 2
    odd_x = place_x % 2

    def in_copy(job):
        source = states if job < 4 else proj
        return pltpu.make_async_copy(
            source.at[pl.ds(16 * (job % 4), 16)], stage_in.at[job % 3], in_sem.at[job % 3]
        )

    for job in range(3):
        in_copy(job).start()

    barrier = pltpu.get_barrier_semaphore()
    for mask in ALL_MASKS:
        pl.semaphore_signal(
            barrier, inc=1, device_id={"dom": flip_bits(me, mask)}, device_id_type=MESH
        )
    mates = []
    for relation in range(1, 4):
        mate_pool = (pool + relation // 2) % 2
        mate_band = (band + relation % 2) % 2
        mates.append((mate_pool, mate_band))
        pl.semaphore_signal(
            barrier,
            inc=1,
            device_id={"pool": mate_pool, "band": mate_band},
            device_id_type=MESH,
        )

    def sign_of(direction, at_edge):
        sign = 1.0 - 2.0 * flips[0, direction].astype(F32)
        return jnp.where(at_edge, sign, jnp.float32(1.0))

    low_x, up_x = sign_of(0, place_x == 0), sign_of(0, place_x == 3)
    low_y, up_y = sign_of(1, place_y == 0), sign_of(1, place_y == 3)
    low_z, up_z = sign_of(2, core == 0), sign_of(2, core == 1)

    def halo_copies(phase, chunk):
        turn = CH * phase + chunk
        source = cur if phase == 0 else nxt
        plan = (
            (send_y.at[chunk, 1 - odd_y], recv_y.at[turn, 0], 2),
            (send_y.at[chunk, odd_y], recv_y.at[turn, 1], 4),
            (send_x.at[chunk, 1 - odd_x], recv_x.at[turn, 0], 8),
            (send_x.at[chunk, odd_x], recv_x.at[turn, 1], 16),
            (source.at[chunk], recv_z.at[turn], 1),
        )
        return [
            pltpu.make_async_remote_copy(
                src_ref=src,
                dst_ref=dst,
                send_sem=send_sem.at[turn, at],
                recv_sem=recv_sem.at[turn, at],
                device_id={"dom": flip_bits(me, mask)},
                device_id_type=MESH,
            )
            for at, (src, dst, mask) in enumerate(plan)
        ]

    lane8 = lax.broadcasted_iota(jnp.int32, (1, 8, 128), 2)

    def enqueue(phase, chunk):
        source = cur if phase == 0 else nxt
        copies = halo_copies(phase, chunk)
        copies[4].start()
        for face, first in ((0, 0), (1, CY - HALO)):
            value = jnp.concatenate(
                [source[chunk, pl.ds(x * CY + first, HALO)] for x in range(XL)], axis=0
            )
            tail = value[YROWS : YROWS + 3]
            for piece in range(15):
                send_y[chunk, face, 3 * piece : 3 * piece + 3] = jnp.where(
                    lane8 < USED, value[3 * piece : 3 * piece + 3], roll(tail, USED - 8 * piece)
                )
        copies[0].start()
        copies[1].start()
        for face, first in ((0, 0), (1, 2 * CY)):
            parts = [
                roll(
                    source[chunk, pl.ds(first + XROWS * group, XROWS)],
                    CZ * group - (GROUPS - 1) * CZ * face,
                )
                for group in range(GROUPS)
            ]
            send_x[chunk, face] = jnp.where(
                lane8 < CZ, parts[0], jnp.where(lane8 < 2 * CZ, parts[1], parts[2])
            )
        copies[2].start()
        copies[3].start()

    def stencil(phase, chunk):
        turn = CH * phase + chunk
        source, target = (cur, nxt) if phase == 0 else (nxt, cur)

        def z_part(half, carry):
            at = pl.ds(half * (ROWS // 2), ROWS // 2)
            left = jnp.concatenate(
                [
                    source[chunk, at].reshape(ROWS * 4, 128),
                    recv_z[turn, at].reshape(ROWS * 4, 128),
                ],
                axis=1,
            )
            high, rest = split(left)
            wide = jnp.dot(high, kz[...], preferred_element_type=F32)
            narrow = jnp.dot(rest, kz[:, :128], preferred_element_type=F32)
            total = (wide[:, :128] + wide[:, 128:] + narrow).reshape(ROWS // 2, 8, 128)
            if phase == 0:
                target[chunk, at] = total
            else:
                target[chunk, at] = total + total - target[chunk, at]
            return carry

        lax.fori_loop(0, 2, z_part, 0)

        for slot_of, sign, first in ((1 - odd_y, low_y, 0), (odd_y, up_y, HALO + CY)):
            rows = []
            tail = jnp.zeros((3, 8, 128), F32)
            for piece in range(15):
                value = recv_y[turn, slot_of, 3 * piece : 3 * piece + 3]
                rows.append(value)
                moved = roll(value, 8 * piece - USED)
                tail = jnp.where((lane8 >= 8 * piece) & (lane8 < 8 * piece + 8), moved, tail)
            rows = jnp.concatenate(rows + [tail], axis=0)
            rows = jnp.where(lane8 < USED, rows * sign, 0.0)
            for x in range(XL):
                ext_y[x, first : first + HALO] = rows[HALO * x : HALO * x + HALO]
        for x in range(XL):
            ext_y[x, HALO : HALO + CY] = source[chunk, x * CY : x * CY + CY]

        for group in range(GROUPS):
            lower = recv_x[turn, 1 - odd_x] * low_x
            ext_x[XROWS * group : XROWS * group + XROWS] = jnp.where(
                lane8 < CZ,
                roll(lower, -CZ * group),
                roll(source[chunk, pl.ds(2 * CY + XROWS * group, XROWS)], CZ),
            )
            upper = recv_x[turn, odd_x] * up_x
            start = (HALO + XL) * CY + XROWS * group
            ext_x[start : start + XROWS] = jnp.where(
                lane8 >= 2 * CZ,
                roll(upper, CZ * (GROUPS - 1 - group)),
                roll(source[chunk, pl.ds(XROWS * group, XROWS)], -CZ),
            )
        ext_x[HALO * CY : (HALO + XL) * CY] = source[chunk]

        def rest_part(step, carry):
            x, half = step // 2, step % 2
            at = pl.ds(x * CY + half * 10, 10)
            column = ext_y[x, pl.ds(half * 10, 10 + 2 * HALO)]
            total = potential[at] * column[HALO : HALO + 10]
            for shift in range(1, HALO + 1):
                pair = column[HALO + shift : HALO + shift + 10] + column[HALO - shift : HALO - shift + 10]
                above = ext_x[pl.ds((x + HALO + shift) * CY + half * 10, 10)]
                below = ext_x[pl.ds((x + HALO - shift) * CY + half * 10, 10)]
                total = total + (SCALE * COEFFS[shift]) * (pair + (above + below))
            if phase == 0:
                target[chunk, at] = target[chunk, at] + total
            else:
                target[chunk, at] = target[chunk, at] + (total + total)
            return carry

        lax.fori_loop(0, 2 * XL, rest_part, 0)

    own_slot = core * 16 + me // 2

    def gather_copies(phase, stage):
        buffer = gather1 if phase == 0 else gather2
        if stage == 0:
            masks, block = Y_MASKS, buffer.at[own_slot]
        elif stage == 1:
            masks, block = X_MASKS, buffer.at[pl.ds(core * 16 + code_x * 4, 4)]
        else:
            masks, block = (1,), buffer.at[pl.ds(core * 16, 16)]
        return [
            pltpu.make_async_remote_copy(
                src_ref=block,
                dst_ref=block,
                send_sem=gsend_sem.at[phase, 3 * stage + at],
                recv_sem=grecv_sem.at[phase, 3 * stage + at],
                device_id={"dom": flip_bits(me, mask)},
                device_id_type=MESH,
            )
            for at, mask in enumerate(masks)
        ]

    def gather_start(phase, stage):
        for copy in gather_copies(phase, stage):
            copy.start()

    def gather_wait(phase, stage):
        for copy in gather_copies(phase, stage):
            copy.wait()

    lane32 = lanes_of(32)

    def coefficients(phase):
        source = cur if phase == 0 else nxt
        buffer = gather1 if phase == 0 else gather2

        def step(pair, total):
            left = jnp.concatenate(
                [source[:, 2 * pair + part].reshape(STATES, 128) for part in range(2)], axis=1
            )
            both = jnp.concatenate(split(left), axis=0)
            return total + lax.dot_general(
                both, pbox[pair], (((1,), (1,)), ((), ())), preferred_element_type=F32
            )

        total = lax.fori_loop(0, PAIRS, step, jnp.zeros((128, 128), F32), unroll=4)
        total = total + roll(total, 64)
        total = total[:STATES] + total[STATES:]
        buffer[own_slot, 0:32] = jnp.where(lane32 < 64, total[:32], total[32:])

    def nonlocal_rows(phase):
        buffer = gather1 if phase == 0 else gather2

        def step(slot, total):
            block = buffer[slot, 0:32]
            pieces = []
            for piece in split(block):
                wide = piece.astype(F32)
                pieces.append(jnp.where(lane32 < 64, wide, 0.0))
                pieces.append(jnp.where(lane32 < 64, 0.0, wide))
            left = jnp.concatenate(pieces, axis=0).astype(BF16)
            return total + lax.dot_general(
                left, same[slot], (((1,), (1,)), ((), ())), preferred_element_type=F32
            )

        total = lax.fori_loop(0, 32, step, jnp.zeros((128, 128), F32), unroll=4)
        weights = (total[:STATES] + total[STATES:]) * coupling_row
        weights = weights * ((phase + 1.0) / HALF_WIDTH)
        left = jnp.concatenate(split(weights), axis=1)

        def spread(pair, carry):
            right = jnp.concatenate([pbox[pair], pbox[pair]], axis=0)
            both = jnp.dot(left, right, preferred_element_type=F32)
            nonloc[:, 2 * pair] = both[:, :128].reshape(CH, 8, 128)
            nonloc[:, 2 * pair + 1] = both[:, 128:].reshape(CH, 8, 128)
            return carry

        lax.fori_loop(0, PAIRS, spread, 0, unroll=4)

    def bring_states(job):
        in_copy(job).wait()

        def block(index, carry):
            for half in range(2):

                def load(group, tile):
                    start = pl.multiple_of(THIRD * group + 640 * index + 128 * tile, 128)
                    return stage_in[job % 3, 8 * half : 8 * half + 8, pl.ds(start, 128)]

                def put(line, row):
                    cur[2 * job + half, LINES * index + line] = row

                rows_from_lines(load, 8, put)
            return carry

        lax.fori_loop(0, BLOCKS, block, 0)
        in_copy(job + 3).start()

    bring_states(0)
    pl.semaphore_wait(barrier, len(ALL_MASKS) + 3)
    enqueue(0, 0)
    enqueue(0, 1)
    bring_states(1)
    enqueue(0, 2)
    bring_states(2)
    bring_states(3)

    kz[0:128] = k_own[...]
    kz[128:256] = (k_low[...].astype(F32) * low_z + k_up[...].astype(F32) * up_z).astype(BF16)

    def potential_block(index, carry):
        def load(group, tile):
            start = pl.multiple_of(THIRD * group + 640 * index + 128 * tile, 128)
            return jnp.broadcast_to(pot[:, pl.ds(start, 128)], (8, 128))

        def put(line, row):
            potential[LINES * index + line] = (row - CENTER) / HALF_WIDTH + 3.0 * SCALE * COEFFS[0]

        rows_from_lines(load, 8, put)
        return carry

    lax.fori_loop(0, BLOCKS, potential_block, 0)

    def diagonal(size):
        return lax.broadcasted_iota(jnp.int32, (size, size), 0) == lax.broadcasted_iota(
            jnp.int32, (size, size), 1
        )

    id_row = ids[...].astype(F32)
    id_pair = jnp.concatenate([id_row, id_row], axis=1)
    id_column = jnp.sum(jnp.where(diagonal(128), id_pair, 0.0), axis=1, keepdims=True)
    all_ids = lax.broadcasted_iota(jnp.int32, (128, 512), 1).astype(F32)
    strength = jnp.sum(
        jnp.where(all_ids == id_column, coupling[...], 0.0), axis=1, keepdims=True
    )
    coupling_row = jnp.sum(jnp.where(diagonal(128), strength, 0.0), axis=0, keepdims=True)
    occ_column = jnp.sum(
        jnp.where(diagonal(STATES), occupation[...], 0.0), axis=1, keepdims=True
    )
    occ_rows[...] = jnp.broadcast_to(occ_column, (STATES, 128)).reshape(CH, 8, 128)
    square[...] = jnp.zeros((ROWS, 8, 128), F32)
    gather1[own_slot, 32:40] = jnp.broadcast_to(id_pair, (8, 128))

    for job in range(4, 8):
        in_copy(job).wait()

        def proj_block(index, carry):
            held = []

            def load(group, tile):
                start = pl.multiple_of(THIRD * group + 640 * index + 128 * tile, 128)
                return stage_in[job % 3, :, pl.ds(start, 128)]

            def put(line, row):
                held.append(row)
                if line % 2 == 1:
                    high, rest = split(jnp.concatenate(held[-2:], axis=1))
                    pair = (LINES // 2) * index + line // 2
                    pbox[pair, 16 * (job - 4) : 16 * (job - 4) + 16] = high
                    pbox[pair, 16 * job : 16 * job + 16] = rest

            rows_from_lines(load, 16, put)
            return carry

        lax.fori_loop(0, BLOCKS, proj_block, 0)
        if job + 3 < 8:
            in_copy(job + 3).start()

    coefficients(0)
    gather_start(0, 0)

    def phase_one(chunk, carry):
        for copy in halo_copies(0, chunk):
            copy.wait()

        @pl.when(chunk == 2)
        def _():
            gather_wait(0, 0)
            gather_start(0, 1)

        @pl.when(chunk == 3)
        def _():
            gather_wait(0, 1)
            gather_start(0, 2)

        @pl.when((chunk >= 1) & (chunk < 6))
        def _():
            enqueue(0, chunk + 2)

        @pl.when(chunk >= 6)
        def _():
            enqueue(1, chunk - 6)

        stencil(0, chunk)

        @pl.when(chunk == 4)
        def _():
            gather_wait(0, 2)

            def compare(slot, inner):
                same[slot] = jnp.where(id_column == gather1[slot, 32:33], 1.0, 0.0).astype(BF16)
                return inner

            lax.fori_loop(0, 32, compare, 0)
            nonlocal_rows(0)

        def finish(done, inner):
            nxt[done] = nxt[done] + nonloc[done]
            return inner

        low = jnp.where(chunk == 4, 0, chunk)
        high = jnp.where(chunk < 4, chunk, chunk + 1)
        lax.fori_loop(low, high, finish, 0)
        return carry

    lax.fori_loop(0, CH, phase_one, 0)

    coefficients(1)
    gather_start(1, 0)

    def phase_two(chunk, carry):
        for copy in halo_copies(1, chunk):
            copy.wait()

        @pl.when(chunk == 1)
        def _():
            gather_wait(1, 0)
            gather_start(1, 1)

        @pl.when(chunk == 2)
        def _():
            gather_wait(1, 1)
            gather_start(1, 2)

        @pl.when(chunk < 6)
        def _():
            enqueue(1, chunk + 2)

        stencil(1, chunk)

        @pl.when(chunk == 3)
        def _():
            gather_wait(1, 2)
            nonlocal_rows(1)

        def finish(done, inner):
            weight = occ_rows[done]

            def block(index, deep):
                at = pl.ds(LINES * index, LINES)
                value = cur[done, at] + nonloc[done, at]
                square[at] = square[at] + value * value * weight

                def put(group, tile, found):
                    start = pl.multiple_of(THIRD * group + 640 * index + 128 * tile, 128)
                    out[pl.ds(pl.multiple_of(8 * done, 8), 8), pl.ds(start, 128)] = found

                lines_from_rows([value[line] for line in range(LINES)], put)
                return deep

            lax.fori_loop(0, BLOCKS, block, 0)
            return inner

        low = jnp.where(chunk == 3, 0, chunk)
        high = jnp.where(chunk < 3, chunk, chunk + 1)
        lax.fori_loop(low, high, finish, 0)
        return carry

    lax.fori_loop(0, CH, phase_two, 0)

    own_numer = numer[0].astype(F32)

    def rho_block(index, carry):
        value = square[pl.ds(LINES * index, LINES)]

        def put(group, tile, found):
            start = pl.multiple_of(THIRD * group + 640 * index + 128 * tile, 128)
            rho[:, pl.ds(start, 128)] = jnp.sum(found, axis=0, keepdims=True) * own_numer

        lines_from_rows([value[line] for line in range(LINES)], put)
        return carry

    lax.fori_loop(0, BLOCKS, rho_block, 0)
    for quarter in range(4):
        start = 128 * (75 * quarter // 2)
        notes[quarter, :, 0:PIECE] = rho[:, start : start + PIECE]
        notes[quarter, :, PIECE:NOTE] = jnp.full((1, 128), own_numer, F32)
    note_copies = [
        pltpu.make_async_remote_copy(
            src_ref=notes.at[2 * mate_pool + mate_band],
            dst_ref=got_notes.at[at],
            send_sem=nsend_sem.at[at],
            recv_sem=nrecv_sem.at[at],
            device_id={"pool": mate_pool, "band": mate_band},
            device_id_type=MESH,
        )
        for at, (mate_pool, mate_band) in enumerate(mates)
    ]
    for copy in note_copies:
        copy.start()
    for copy in note_copies:
        copy.wait()
    total = notes[2 * pool + band] + got_notes[0] + got_notes[1] + got_notes[2]
    count = total[:, PIECE : PIECE + 1] * 0.5
    total = jnp.where(band == 1, total[:, 64:PIECE], total[:, : PIECE - 64])
    dens[...] = total / count


def body(
    states_in, bloch_flip, kweight_num, local_pot, proj_values, proj_ids, coupling, occupation
):
    k_own, k_low, k_up = z_matrices()
    vmem = pl.BlockSpec(memory_space=pltpu.VMEM)
    smem = pl.BlockSpec(memory_space=pltpu.SMEM)
    hbm = pl.BlockSpec(memory_space=pl.ANY)
    dma = pltpu.SemaphoreType.DMA
    out, dens = pl.pallas_call(
        kernel,
        out_shape=(
            pltpu.VMEM((STATES, CELLS), F32),
            jax.ShapeDtypeStruct((1, CELLS // 4), F32),
        ),
        in_specs=[hbm, smem, smem, vmem, hbm, vmem, vmem, vmem, vmem, vmem, vmem],
        out_specs=(vmem, vmem),
        scratch_shapes=[
            pltpu.VMEM((CH, ROWS, 8, 128), F32),
            pltpu.VMEM((CH, ROWS, 8, 128), F32),
            pltpu.VMEM((CH, ROWS, 8, 128), F32),
            pltpu.VMEM((PAIRS, 2 * SLOTS, 256), BF16),
            pltpu.VMEM((CH, 2, YROWS, 8, 128), F32),
            pltpu.VMEM((CH, 2, XROWS, 8, 128), F32),
            pltpu.VMEM((2 * CH, 2, YROWS, 8, 128), F32),
            pltpu.VMEM((2 * CH, 2, XROWS, 8, 128), F32),
            pltpu.VMEM((2 * CH, ROWS, 8, 128), F32),
            pltpu.VMEM(((XL + 2 * HALO) * CY, 8, 128), F32),
            pltpu.VMEM((XL, CY + 2 * HALO, 8, 128), F32),
            pltpu.VMEM((ROWS, 8, 128), F32),
            pltpu.VMEM((256, 256), BF16),
            pltpu.VMEM((32, 40, 128), F32),
            pltpu.VMEM((32, 32, 128), F32),
            pltpu.VMEM((32, 128, 128), BF16),
            pltpu.VMEM((CH, 8, 128), F32),
            pltpu.VMEM((ROWS, 8, 128), F32),
            pltpu.VMEM((1, CELLS), F32),
            pltpu.VMEM((4, 1, NOTE), F32),
            pltpu.VMEM((3, 1, NOTE), F32),
            pltpu.VMEM((3, 16, CELLS), F32),
            dma((3,)),
            dma((2 * CH, 5)),
            dma((2 * CH, 5)),
            dma((2, 9)),
            dma((2, 9)),
            dma((3,)),
            dma((3,)),
        ],
        compiler_params=pltpu.CompilerParams(
            collective_id=0, has_side_effects=True, vmem_limit_bytes=58 << 20
        ),
    )(
        states_in[0, 0],
        bloch_flip,
        kweight_num,
        local_pot,
        proj_values[0],
        proj_ids,
        coupling[None],
        occupation[None],
        k_own,
        k_low,
        k_up,
    )
    return out[None, None], dens


def solution(mesh):
    placed = (
        P("pool", "dom", "band", None),
        P("pool", None),
        P("pool"),
        P("dom", None),
        P("dom", None, None),
        P("dom", None),
        P(),
        P("band"),
    )
    return jax.shard_map(
        body,
        mesh=mesh,
        in_specs=placed,
        out_specs=(P("pool", "dom", "band", None), P("dom", ("pool", "band"))),
        check_vma=False,
    )
```

```python
import jax
import jax.numpy as jnp
import numpy as np
from jax import lax
from jax.experimental import pallas as pl
from jax.experimental.pallas import tpu as pltpu
from jax.sharding import PartitionSpec as P

MESH = pl.DeviceIdType.MESH
F32 = jnp.float32
BF16 = jnp.bfloat16

HALO = 6
CX = 24
CY = 20
CZ = 40
CELLS = CX * CY * CZ
COEFFS = (
    -5369.0 / 1800.0,
    12.0 / 7.0,
    -15.0 / 56.0,
    10.0 / 189.0,
    -1.0 / 112.0,
    2.0 / 1925.0,
    -1.0 / 16632.0,
)
CENTER = 14.0
HALF_WIDTH = 10.0
SCALE = -0.5 / HALF_WIDTH

GROUPS = 3
XL = CX // GROUPS
ROWS = XL * CY
USED = GROUPS * CZ
THIRD = CELLS // GROUPS
BLOCKS = 10
LINES = 16
STATES = 64
CH = 8
SLOTS = 64
PAIRS = ROWS // 2
YROWS = 45
XROWS = 40
PIECE = 4864

Y_MASKS = (2, 4, 6)
X_MASKS = (8, 16, 24)
ALL_MASKS = (1,) + Y_MASKS + X_MASKS


def z_matrices():
    own = np.zeros((128, 128), np.float64)
    low = np.zeros((128, 128), np.float64)
    up = np.zeros((128, 128), np.float64)
    for group in range(GROUPS):
        for z in range(CZ):
            for shift in range(1, HALO + 1):
                for source in (z + shift, z - shift):
                    target = own if 0 <= source < CZ else (low if source < 0 else up)
                    target[group * CZ + source % CZ, group * CZ + z] += SCALE * COEFFS[shift]
    pairs = []
    for matrix in (own, low, up):
        high = jnp.asarray(matrix, F32).astype(BF16)
        rest = (jnp.asarray(matrix, F32) - high.astype(F32)).astype(BF16)
        pairs.append(jnp.concatenate([high, rest], axis=1))
    return pairs


def flip_bits(me, mask):
    other = me
    for bit in (1, 2, 4, 8, 16):
        if mask & bit:
            other = other + bit * (1 - 2 * ((me // bit) % 2))
    return other


def lanes_of(rows):
    return lax.broadcasted_iota(jnp.int32, (rows, 128), 1)


def roll(value, shift):
    shift = shift % 128
    if shift == 0:
        return value
    return pltpu.roll(value, shift, value.ndim - 1)


def split(value):
    high = value.astype(BF16)
    return high, (value - high.astype(F32)).astype(BF16)


def rows_from_lines(load, count, put):
    lane = lanes_of(count)
    tiles = [[load(group, tile) for tile in range(5)] for group in range(GROUPS)]
    for line in range(LINES):
        tile, offset = divmod(CZ * line, 128)
        parts = []
        for group in range(GROUPS):
            value = tiles[group][tile]
            if offset + CZ > 128:
                value = jnp.where(lane >= offset, value, tiles[group][tile + 1])
            parts.append(roll(value, CZ * group - offset))
        row = jnp.where(lane < CZ, parts[0], jnp.where(lane < 2 * CZ, parts[1], parts[2]))
        put(line, jnp.where(lane < USED, row, 0.0))


def lines_from_rows(rows, put):
    lane = lanes_of(8)
    for group in range(GROUPS):
        for tile in range(5):
            first, offset = divmod(128 * tile, CZ)
            value = None
            for step in range(4):
                part = roll(rows[first + step], CZ * step - offset - CZ * group)
                value = part if step == 0 else jnp.where(lane < CZ * step - offset, value, part)
            put(group, tile, value)


def kernel(
    states,
    flips,
    numer,
    pot,
    proj,
    ids,
    coupling,
    occupation,
    k_own,
    k_low,
    k_up,
    out,
    dens,
    cur,
    nxt,
    nonloc,
    pbox,
    send_y,
    send_x,
    recv_y,
    recv_x,
    recv_z,
    ext_x,
    ext_y,
    halo_y,
    potential,
    kz,
    gather1,
    gather2,
    same,
    occ_rows,
    rho,
    count_note,
    got_notes,
    stage_in,
    in_sem,
    send_sem,
    recv_sem,
    gsend_sem,
    grecv_sem,
    nsend_sem,
    nrecv_sem,
):
    me = lax.axis_index("dom")
    pool = lax.axis_index("pool")
    band = lax.axis_index("band")
    core = me % 2
    code_y = (me // 2) % 4
    code_x = me // 8

    def place_of(code):
        return code + (code // 2) * (1 - 2 * (code % 2))

    place_y = place_of(code_y)
    place_x = place_of(code_x)
    odd_y = place_y % 2
    odd_x = place_x % 2

    def state_copy(chunk):
        slot, half = (chunk // 2) % 3, chunk % 2
        return pltpu.make_async_copy(
            states.at[pl.ds(8 * chunk, 8)],
            stage_in.at[slot, pl.ds(8 * half, 8)],
            in_sem.at[slot, half],
        )

    def proj_copy(job):
        slot = (job + 1) % 3
        return pltpu.make_async_copy(
            proj.at[pl.ds(16 * job, 16)], stage_in.at[slot], in_sem.at[slot, 0]
        )

    for chunk in range(6):
        state_copy(chunk).start()

    barrier = pltpu.get_barrier_semaphore()
    for mask in ALL_MASKS:
        pl.semaphore_signal(
            barrier, inc=1, device_id={"dom": flip_bits(me, mask)}, device_id_type=MESH
        )
    mates = []
    for relation in range(1, 4):
        mate_pool = (pool + relation // 2) % 2
        mate_band = (band + relation % 2) % 2
        mates.append((mate_pool, mate_band))
        pl.semaphore_signal(
            barrier,
            inc=1,
            device_id={"pool": mate_pool, "band": mate_band},
            device_id_type=MESH,
        )

    def sign_of(direction, at_edge):
        sign = 1.0 - 2.0 * flips[0, direction].astype(F32)
        return jnp.where(at_edge, sign, jnp.float32(1.0))

    low_x, up_x = sign_of(0, place_x == 0), sign_of(0, place_x == 3)
    low_y, up_y = sign_of(1, place_y == 0), sign_of(1, place_y == 3)
    low_z, up_z = sign_of(2, core == 0), sign_of(2, core == 1)

    def halo_copies(phase, chunk, wanted):
        turn = CH * phase + chunk
        source = cur if phase == 0 else nxt
        plan = (
            (send_y.at[chunk, 1 - odd_y], recv_y.at[turn, 0], 2),
            (send_y.at[chunk, odd_y], recv_y.at[turn, 1], 4),
            (send_x.at[chunk, 1 - odd_x], recv_x.at[turn, 0], 8),
            (send_x.at[chunk, odd_x], recv_x.at[turn, 1], 16),
            (source.at[chunk], recv_z.at[turn], 1),
        )
        return [
            pltpu.make_async_remote_copy(
                src_ref=src,
                dst_ref=dst,
                send_sem=send_sem.at[turn, at],
                recv_sem=recv_sem.at[turn, at],
                device_id={"dom": flip_bits(me, mask)},
                device_id_type=MESH,
            )
            for at, (src, dst, mask) in enumerate(plan)
            if at in wanted
        ]

    lane8 = lax.broadcasted_iota(jnp.int32, (1, 8, 128), 2)

    def enqueue(phase, chunk):
        source = cur if phase == 0 else nxt
        copies = halo_copies(phase, chunk, range(5))
        copies[4].start()
        for face, first in ((0, 0), (1, CY - HALO)):
            value = jnp.concatenate(
                [source[chunk, pl.ds(x * CY + first, HALO)] for x in range(XL)], axis=0
            )
            tail = value[YROWS : YROWS + 3]
            for piece in range(15):
                send_y[chunk, face, 3 * piece : 3 * piece + 3] = jnp.where(
                    lane8 < USED, value[3 * piece : 3 * piece + 3], roll(tail, USED - 8 * piece)
                )
        copies[0].start()
        copies[1].start()
        for face, first in ((0, 0), (1, 2 * CY)):
            parts = [
                roll(
                    source[chunk, pl.ds(first + XROWS * group, XROWS)],
                    CZ * group - (GROUPS - 1) * CZ * face,
                )
                for group in range(GROUPS)
            ]
            send_x[chunk, face] = jnp.where(
                lane8 < CZ, parts[0], jnp.where(lane8 < 2 * CZ, parts[1], parts[2])
            )
        copies[2].start()
        copies[3].start()

    def inner_part(phase, chunk):
        turn = CH * phase + chunk
        source, target = (cur, nxt) if phase == 0 else (nxt, cur)

        def z_part(half, carry):
            at = pl.ds(half * (ROWS // 2), ROWS // 2)
            left = jnp.concatenate(
                [
                    source[chunk, at].reshape(ROWS * 4, 128),
                    recv_z[turn, at].reshape(ROWS * 4, 128),
                ],
                axis=1,
            )
            high, rest = split(left)
            wide = jnp.dot(high, kz[...], preferred_element_type=F32)
            narrow = jnp.dot(rest, kz[:, :128], preferred_element_type=F32)
            total = (wide[:, :128] + wide[:, 128:] + narrow).reshape(ROWS // 2, 8, 128)
            if phase == 0:
                target[chunk, at] = total
            else:
                target[chunk, at] = total + total - target[chunk, at]
            return carry

        lax.fori_loop(0, 2, z_part, 0)

        for x in range(XL):
            ext_y[x, HALO : HALO + CY] = source[chunk, x * CY : x * CY + CY]

        for group in range(GROUPS):
            lower = recv_x[turn, 1 - odd_x] * low_x
            ext_x[XROWS * group : XROWS * group + XROWS] = jnp.where(
                lane8 < CZ,
                roll(lower, -CZ * group),
                roll(source[chunk, pl.ds(2 * CY + XROWS * group, XROWS)], CZ),
            )
            upper = recv_x[turn, odd_x] * up_x
            start = (HALO + XL) * CY + XROWS * group
            ext_x[start : start + XROWS] = jnp.where(
                lane8 >= 2 * CZ,
                roll(upper, CZ * (GROUPS - 1 - group)),
                roll(source[chunk, pl.ds(XROWS * group, XROWS)], -CZ),
            )
        ext_x[HALO * CY : (HALO + XL) * CY] = source[chunk]

        def rest_part(step, carry):
            x, half = step // 2, step % 2
            at = pl.ds(x * CY + half * 10, 10)
            column = ext_y[x, pl.ds(half * 10, 10 + 2 * HALO)]
            total = potential[at] * column[HALO : HALO + 10]
            for shift in range(1, HALO + 1):
                pair = column[HALO + shift : HALO + shift + 10] + column[HALO - shift : HALO - shift + 10]
                above = ext_x[pl.ds((x + HALO + shift) * CY + half * 10, 10)]
                below = ext_x[pl.ds((x + HALO - shift) * CY + half * 10, 10)]
                total = total + (SCALE * COEFFS[shift]) * (pair + (above + below))
            if phase == 0:
                target[chunk, at] = target[chunk, at] + total
            else:
                target[chunk, at] = target[chunk, at] + (total + total)
            return carry

        lax.fori_loop(0, 2 * XL, rest_part, 0)

    def y_halo_part(phase, chunk):
        turn = CH * phase + chunk
        target = nxt if phase == 0 else cur
        scale = SCALE * (phase + 1.0)
        for face, slot_of, sign in ((0, 1 - odd_y, low_y), (1, odd_y, up_y)):
            tail = jnp.zeros((3, 8, 128), F32)
            for piece in range(15):
                value = recv_y[turn, slot_of, 3 * piece : 3 * piece + 3]
                halo_y[face, 3 * piece : 3 * piece + 3] = value * sign
                moved = roll(value, 8 * piece - USED)
                tail = jnp.where((lane8 >= 8 * piece) & (lane8 < 8 * piece + 8), moved, tail)
            halo_y[face, YROWS : YROWS + 3] = tail * sign

        def column(x, carry):
            low = halo_y[0, pl.ds(HALO * x, HALO)]
            up = halo_y[1, pl.ds(HALO * x, HALO)]
            first, last = [], []
            for y in range(HALO):
                first.append(
                    sum(
                        (scale * COEFFS[shift]) * low[HALO + y - shift]
                        for shift in range(y + 1, HALO + 1)
                    )
                )
                last.append(
                    sum(
                        (scale * COEFFS[shift]) * up[y + shift - HALO]
                        for shift in range(HALO - y, HALO + 1)
                    )
                )
            at = pl.ds(x * CY, HALO)
            target[chunk, at] = target[chunk, at] + jnp.stack(first)
            at = pl.ds(x * CY + CY - HALO, HALO)
            target[chunk, at] = target[chunk, at] + jnp.stack(last)
            return carry

        lax.fori_loop(0, XL, column, 0, unroll=2)

    own_slot = core * 16 + me // 2

    def gather_copies(phase, stage):
        buffer = gather1 if phase == 0 else gather2
        if stage == 0:
            masks, block = Y_MASKS, buffer.at[own_slot]
        elif stage == 1:
            masks, block = X_MASKS, buffer.at[pl.ds(core * 16 + code_x * 4, 4)]
        else:
            masks, block = (1,), buffer.at[pl.ds(core * 16, 16)]
        return [
            pltpu.make_async_remote_copy(
                src_ref=block,
                dst_ref=block,
                send_sem=gsend_sem.at[phase, 3 * stage + at],
                recv_sem=grecv_sem.at[phase, 3 * stage + at],
                device_id={"dom": flip_bits(me, mask)},
                device_id_type=MESH,
            )
            for at, mask in enumerate(masks)
        ]

    def gather_start(phase, stage):
        for copy in gather_copies(phase, stage):
            copy.start()

    def gather_wait(phase, stage):
        for copy in gather_copies(phase, stage):
            copy.wait()

    lane32 = lanes_of(32)

    def coefficients(phase):
        source = cur if phase == 0 else nxt
        buffer = gather1 if phase == 0 else gather2

        def step(pair, total):
            left = jnp.concatenate(
                [source[:, 2 * pair + part].reshape(STATES, 128) for part in range(2)], axis=1
            )
            both = jnp.concatenate(split(left), axis=0)
            return total + lax.dot_general(
                both, pbox[pair], (((1,), (1,)), ((), ())), preferred_element_type=F32
            )

        total = lax.fori_loop(0, PAIRS, step, jnp.zeros((128, 128), F32), unroll=4)
        total = total + roll(total, 64)
        total = total[:STATES] + total[STATES:]
        buffer[own_slot, 0:32] = jnp.where(lane32 < 64, total[:32], total[32:])

    def nonlocal_rows(phase):
        buffer = gather1 if phase == 0 else gather2

        def step(slot, total):
            block = buffer[slot, 0:32]
            pieces = []
            for piece in split(block):
                wide = piece.astype(F32)
                pieces.append(jnp.where(lane32 < 64, wide, 0.0))
                pieces.append(jnp.where(lane32 < 64, 0.0, wide))
            left = jnp.concatenate(pieces, axis=0).astype(BF16)
            return total + lax.dot_general(
                left, same[slot], (((1,), (1,)), ((), ())), preferred_element_type=F32
            )

        total = lax.fori_loop(0, 32, step, jnp.zeros((128, 128), F32), unroll=4)
        weights = (total[:STATES] + total[STATES:]) * coupling_row
        weights = weights * ((phase + 1.0) / HALF_WIDTH)
        left = jnp.concatenate(split(weights), axis=1)

        def spread(pair, carry):
            right = jnp.concatenate([pbox[pair], pbox[pair]], axis=0)
            both = jnp.dot(left, right, preferred_element_type=F32)
            nonloc[:, 2 * pair] = both[:, :128].reshape(CH, 8, 128)
            nonloc[:, 2 * pair + 1] = both[:, 128:].reshape(CH, 8, 128)
            return carry

        lax.fori_loop(0, PAIRS, spread, 0, unroll=4)

    def bring_states(chunk):
        state_copy(chunk).wait()
        slot, half = (chunk // 2) % 3, chunk % 2

        def block(index, carry):
            def load(group, tile):
                start = pl.multiple_of(THIRD * group + 640 * index + 128 * tile, 128)
                return stage_in[slot, 8 * half : 8 * half + 8, pl.ds(start, 128)]

            def put(line, row):
                cur[chunk, LINES * index + line] = row

            rows_from_lines(load, 8, put)
            return carry

        lax.fori_loop(0, BLOCKS, block, 0, unroll=5)

    bring_states(0)
    pl.semaphore_wait(barrier, len(ALL_MASKS) + 3)
    enqueue(0, 0)
    bring_states(1)
    enqueue(0, 1)
    state_copy(6).start()
    state_copy(7).start()
    bring_states(2)
    enqueue(0, 2)
    own_numer = numer[0].astype(F32)
    count_note[0] = jnp.full((1, 128), own_numer, F32)
    count_copy = pltpu.make_async_remote_copy(
        src_ref=count_note.at[0],
        dst_ref=count_note.at[1],
        send_sem=nsend_sem.at[3],
        recv_sem=nrecv_sem.at[3],
        device_id={"pool": (pool + 1) % 2, "band": band},
        device_id_type=MESH,
    )
    count_copy.start()
    bring_states(3)
    proj_copy(0).start()
    bring_states(4)
    bring_states(5)
    proj_copy(1).start()
    bring_states(6)
    bring_states(7)
    proj_copy(2).start()

    def diagonal(size):
        return lax.broadcasted_iota(jnp.int32, (size, size), 0) == lax.broadcasted_iota(
            jnp.int32, (size, size), 1
        )

    id_row = ids[...].astype(F32)
    id_pair = jnp.concatenate([id_row, id_row], axis=1)
    id_column = jnp.sum(jnp.where(diagonal(128), id_pair, 0.0), axis=1, keepdims=True)
    gather1[own_slot, 32:40] = jnp.broadcast_to(id_pair, (8, 128))

    for job in range(4):
        proj_copy(job).wait()

        def proj_block(index, carry):
            held = []

            def load(group, tile):
                start = pl.multiple_of(THIRD * group + 640 * index + 128 * tile, 128)
                return stage_in[(job + 1) % 3, :, pl.ds(start, 128)]

            def put(line, row):
                held.append(row)
                if line % 2 == 1:
                    high, rest = split(jnp.concatenate(held[-2:], axis=1))
                    pair = (LINES // 2) * index + line // 2
                    pbox[pair, 16 * job : 16 * job + 16] = high
                    pbox[pair, SLOTS + 16 * job : SLOTS + 16 * job + 16] = rest

            rows_from_lines(load, 16, put)
            return carry

        lax.fori_loop(0, BLOCKS, proj_block, 0, unroll=5)
        if job == 0:
            proj_copy(3).start()

    coefficients(0)
    gather_start(0, 0)
    enqueue(0, 3)

    for x in range(XL):
        ext_y[x, 0:HALO] = jnp.zeros((HALO, 8, 128), F32)
        ext_y[x, HALO + CY :] = jnp.zeros((HALO, 8, 128), F32)
    kz[0:128] = k_own[...]
    kz[128:256] = (k_low[...].astype(F32) * low_z + k_up[...].astype(F32) * up_z).astype(BF16)

    def potential_block(index, carry):
        def load(group, tile):
            start = pl.multiple_of(THIRD * group + 640 * index + 128 * tile, 128)
            return jnp.broadcast_to(pot[:, pl.ds(start, 128)], (8, 128))

        def put(line, row):
            potential[LINES * index + line] = (row - CENTER) / HALF_WIDTH + 3.0 * SCALE * COEFFS[0]

        rows_from_lines(load, 8, put)
        return carry

    lax.fori_loop(0, BLOCKS, potential_block, 0, unroll=5)

    all_ids = lax.broadcasted_iota(jnp.int32, (128, 512), 1).astype(F32)
    strength = jnp.sum(
        jnp.where(all_ids == id_column, coupling[...], 0.0), axis=1, keepdims=True
    )
    coupling_row = jnp.sum(jnp.where(diagonal(128), strength, 0.0), axis=0, keepdims=True)
    occ_column = jnp.sum(
        jnp.where(diagonal(STATES), occupation[...], 0.0), axis=1, keepdims=True
    )
    occ_rows[...] = jnp.broadcast_to(occ_column * own_numer, (STATES, 128)).reshape(CH, 8, 128)
    rho[...] = jnp.zeros((1, CELLS), F32)

    def wait_y(phase, chunk):
        for copy in halo_copies(phase, chunk, (0, 1)):
            copy.wait()

    def wait_rest(phase, chunk):
        for copy in halo_copies(phase, chunk, (2, 3, 4)):
            copy.wait()

    def phase_one(chunk, carry):
        wait_y(0, chunk)

        @pl.when(chunk == 2)
        def _():
            gather_wait(0, 0)
            gather_start(0, 1)

        @pl.when(chunk == 3)
        def _():
            gather_wait(0, 1)
            gather_start(0, 2)

        @pl.when((chunk >= 2) & (chunk < 6))
        def _():
            enqueue(0, chunk + 2)

        @pl.when(chunk >= 6)
        def _():
            enqueue(1, chunk - 6)

        y_halo_part(0, chunk)

        @pl.when(chunk == 4)
        def _():
            gather_wait(0, 2)

            def compare(slot, inner):
                same[slot] = jnp.where(id_column == gather1[slot, 32:33], 1.0, 0.0).astype(BF16)
                return inner

            lax.fori_loop(0, 32, compare, 0)
            nonlocal_rows(0)

        def finish(done, inner):
            nxt[done] = nxt[done] + nonloc[done]
            return inner

        low = jnp.where(chunk == 4, 0, chunk)
        high = jnp.where(chunk < 4, chunk, chunk + 1)
        lax.fori_loop(low, high, finish, 0)

        @pl.when(chunk < CH - 1)
        def _():
            wait_rest(0, chunk + 1)
            inner_part(0, chunk + 1)

        return carry

    wait_rest(0, 0)
    inner_part(0, 0)
    lax.fori_loop(0, CH, phase_one, 0)

    coefficients(1)
    gather_start(1, 0)

    def phase_two(chunk, carry):
        wait_y(1, chunk)

        @pl.when(chunk == 1)
        def _():
            gather_wait(1, 0)
            gather_start(1, 1)

        @pl.when(chunk == 2)
        def _():
            gather_wait(1, 1)
            gather_start(1, 2)

        @pl.when(chunk < 6)
        def _():
            enqueue(1, chunk + 2)

        y_halo_part(1, chunk)

        @pl.when(chunk == 3)
        def _():
            gather_wait(1, 2)
            nonlocal_rows(1)

        def finish(done, inner):
            weight = occ_rows[done]

            def block(index, deep):
                at = pl.ds(LINES * index, LINES)
                value = cur[done, at] + nonloc[done, at]
                def put(group, tile, found):
                    start = pl.multiple_of(THIRD * group + 640 * index + 128 * tile, 128)
                    out[pl.ds(pl.multiple_of(8 * done, 8), 8), pl.ds(start, 128)] = found
                    rho[:, pl.ds(start, 128)] = rho[:, pl.ds(start, 128)] + jnp.sum(
                        found * found * weight, axis=0, keepdims=True
                    )

                lines_from_rows([value[line] for line in range(LINES)], put)
                return deep

            lax.fori_loop(0, BLOCKS, block, 0, unroll=5)
            return inner

        low = jnp.where(chunk == 3, 0, chunk)
        high = jnp.where(chunk < 3, chunk, chunk + 1)
        lax.fori_loop(low, high, finish, 0)

        @pl.when(chunk < CH - 1)
        def _():
            wait_rest(1, chunk + 1)
            inner_part(1, chunk + 1)

        return carry

    wait_rest(1, 0)
    inner_part(1, 0)
    lax.fori_loop(0, CH, phase_two, 0)

    def quarter_of(mate_pool, mate_band):
        start = pl.multiple_of(128 * (75 * (2 * mate_pool + mate_band) // 2), 128)
        return pl.ds(start, PIECE)

    note_copies = [
        pltpu.make_async_remote_copy(
            src_ref=rho.at[:, quarter_of(mate_pool, mate_band)],
            dst_ref=got_notes.at[at],
            send_sem=nsend_sem.at[at],
            recv_sem=nrecv_sem.at[at],
            device_id={"pool": mate_pool, "band": mate_band},
            device_id_type=MESH,
        )
        for at, (mate_pool, mate_band) in enumerate(mates)
    ]
    for copy in note_copies[::-1]:
        copy.start()
    count_copy.wait()
    total_numer = count_note[0] + count_note[1]
    for copy in note_copies:
        copy.wait()
    total = rho[:, quarter_of(pool, band)] + got_notes[0] + got_notes[1] + got_notes[2]
    total = jnp.where(band == 1, total[:, 64:PIECE], total[:, : PIECE - 64])
    dens[...] = total / total_numer[:, 0:1]


def body(
    states_in, bloch_flip, kweight_num, local_pot, proj_values, proj_ids, coupling, occupation
):
    k_own, k_low, k_up = z_matrices()
    vmem = pl.BlockSpec(memory_space=pltpu.VMEM)
    smem = pl.BlockSpec(memory_space=pltpu.SMEM)
    hbm = pl.BlockSpec(memory_space=pl.ANY)
    dma = pltpu.SemaphoreType.DMA
    out, dens = pl.pallas_call(
        kernel,
        out_shape=(
            pltpu.VMEM((STATES, CELLS), F32),
            pltpu.VMEM((1, CELLS // 4), F32),
        ),
        in_specs=[hbm, smem, smem, vmem, hbm, vmem, vmem, vmem, vmem, vmem, vmem],
        out_specs=(vmem, vmem),
        scratch_shapes=[
            pltpu.VMEM((CH, ROWS, 8, 128), F32),
            pltpu.VMEM((CH, ROWS, 8, 128), F32),
            pltpu.VMEM((CH, ROWS, 8, 128), F32),
            pltpu.VMEM((PAIRS, 2 * SLOTS, 256), BF16),
            pltpu.VMEM((CH, 2, YROWS, 8, 128), F32),
            pltpu.VMEM((CH, 2, XROWS, 8, 128), F32),
            pltpu.VMEM((2 * CH, 2, YROWS, 8, 128), F32),
            pltpu.VMEM((2 * CH, 2, XROWS, 8, 128), F32),
            pltpu.VMEM((2 * CH, ROWS, 8, 128), F32),
            pltpu.VMEM(((XL + 2 * HALO) * CY, 8, 128), F32),
            pltpu.VMEM((XL, CY + 2 * HALO, 8, 128), F32),
            pltpu.VMEM((2, XL * HALO, 8, 128), F32),
            pltpu.VMEM((ROWS, 8, 128), F32),
            pltpu.VMEM((256, 256), BF16),
            pltpu.VMEM((32, 40, 128), F32),
            pltpu.VMEM((32, 32, 128), F32),
            pltpu.VMEM((32, 128, 128), BF16),
            pltpu.VMEM((CH, 8, 128), F32),
            pltpu.VMEM((1, CELLS), F32),
            pltpu.VMEM((2, 1, 128), F32),
            pltpu.VMEM((3, 1, PIECE), F32),
            pltpu.VMEM((3, 16, CELLS), F32),
            dma((3, 2)),
            dma((2 * CH, 5)),
            dma((2 * CH, 5)),
            dma((2, 9)),
            dma((2, 9)),
            dma((4,)),
            dma((4,)),
        ],
        compiler_params=pltpu.CompilerParams(
            collective_id=0, has_side_effects=True, vmem_limit_bytes=58 << 20
        ),
    )(
        states_in[0, 0],
        bloch_flip,
        kweight_num,
        local_pot,
        proj_values[0],
        proj_ids,
        coupling[None],
        occupation[None],
        k_own,
        k_low,
        k_up,
    )
    return out[None, None], dens


def solution(mesh):
    placed = (
        P("pool", "dom", "band", None),
        P("pool", None),
        P("pool"),
        P("dom", None),
        P("dom", None, None),
        P("dom", None),
        P(),
        P("band"),
    )
    return jax.shard_map(
        body,
        mesh=mesh,
        in_specs=placed,
        out_specs=(P("pool", "dom", "band", None), P("dom", ("pool", "band"))),
        check_vma=False,
    )
```

```python
import jax
import jax.numpy as jnp
import numpy as np
from jax import lax
from jax.experimental import pallas as pl
from jax.experimental.pallas import tpu as pltpu
from jax.sharding import PartitionSpec as P

MESH = pl.DeviceIdType.MESH
F32 = jnp.float32
BF16 = jnp.bfloat16

HALO = 6
CX = 24
CY = 20
CZ = 40
CELLS = CX * CY * CZ
COEFFS = (
    -5369.0 / 1800.0,
    12.0 / 7.0,
    -15.0 / 56.0,
    10.0 / 189.0,
    -1.0 / 112.0,
    2.0 / 1925.0,
    -1.0 / 16632.0,
)
CENTER = 14.0
HALF_WIDTH = 10.0
SCALE = -0.5 / HALF_WIDTH

GROUPS = 3
XL = CX // GROUPS
ROWS = XL * CY
USED = GROUPS * CZ
THIRD = CELLS // GROUPS
BLOCKS = 10
LINES = 16
STATES = 64
CH = 8
SLOTS = 64
PAIRS = ROWS // 2
YROWS = 45
XROWS = 40
PIECE = 4864

Y_MASKS = (2, 4, 6)
X_MASKS = (8, 16, 24)
ALL_MASKS = (1,) + Y_MASKS + X_MASKS


def z_matrices():
    own = np.zeros((128, 128), np.float64)
    low = np.zeros((128, 128), np.float64)
    up = np.zeros((128, 128), np.float64)
    for group in range(GROUPS):
        for z in range(CZ):
            for shift in range(1, HALO + 1):
                for source in (z + shift, z - shift):
                    target = own if 0 <= source < CZ else (low if source < 0 else up)
                    target[group * CZ + source % CZ, group * CZ + z] += SCALE * COEFFS[shift]
    pairs = []
    for matrix in (own, low, up):
        high = jnp.asarray(matrix, F32).astype(BF16)
        rest = (jnp.asarray(matrix, F32) - high.astype(F32)).astype(BF16)
        pairs.append(jnp.concatenate([high, rest], axis=1))
    return pairs


def flip_bits(me, mask):
    other = me
    for bit in (1, 2, 4, 8, 16):
        if mask & bit:
            other = other + bit * (1 - 2 * ((me // bit) % 2))
    return other


def lanes_of(rows):
    return lax.broadcasted_iota(jnp.int32, (rows, 128), 1)


def roll(value, shift):
    shift = shift % 128
    if shift == 0:
        return value
    return pltpu.roll(value, shift, value.ndim - 1)


def split(value):
    high = value.astype(BF16)
    return high, (value - high.astype(F32)).astype(BF16)


def rows_from_lines(load, count, put):
    lane = lanes_of(count)
    tiles = [[load(group, tile) for tile in range(5)] for group in range(GROUPS)]
    for line in range(LINES):
        tile, offset = divmod(CZ * line, 128)
        parts = []
        for group in range(GROUPS):
            value = tiles[group][tile]
            if offset + CZ > 128:
                value = jnp.where(lane >= offset, value, tiles[group][tile + 1])
            parts.append(roll(value, CZ * group - offset))
        row = jnp.where(lane < CZ, parts[0], jnp.where(lane < 2 * CZ, parts[1], parts[2]))
        put(line, jnp.where(lane < USED, row, 0.0))


def lines_from_rows(rows, put):
    lane = lanes_of(8)
    for group in range(GROUPS):
        for tile in range(5):
            first, offset = divmod(128 * tile, CZ)
            value = None
            for step in range(4):
                part = roll(rows[first + step], CZ * step - offset - CZ * group)
                value = part if step == 0 else jnp.where(lane < CZ * step - offset, value, part)
            put(group, tile, value)


def kernel(
    states,
    flips_in,
    numer_in,
    pot_in,
    proj,
    ids_in,
    coupling_in,
    occupation_in,
    k_own_in,
    k_low_in,
    k_up_in,
    out,
    dens,
    cur,
    nxt,
    nonloc,
    pbox,
    send_y,
    send_x,
    recv_y,
    recv_x,
    recv_z,
    ext_x,
    ext_y,
    halo_y,
    potential,
    kz,
    gather1,
    gather2,
    same,
    occ_rows,
    rho,
    count_note,
    got_notes,
    stage_in,
    flips,
    numer,
    pot,
    ids,
    coupling,
    occupation,
    k_own,
    k_low,
    k_up,
    in_sem,
    small_sem,
    send_sem,
    recv_sem,
    gsend_sem,
    grecv_sem,
    nsend_sem,
    nrecv_sem,
):
    me = lax.axis_index("dom")
    pool = lax.axis_index("pool")
    band = lax.axis_index("band")
    core = me % 2
    code_y = (me // 2) % 4
    code_x = me // 8

    def place_of(code):
        return code + (code // 2) * (1 - 2 * (code % 2))

    place_y = place_of(code_y)
    place_x = place_of(code_x)
    odd_y = place_y % 2
    odd_x = place_x % 2

    def state_copy(chunk):
        slot, half = (chunk // 2) % 3, chunk % 2
        return pltpu.make_async_copy(
            states.at[pl.ds(8 * chunk, 8)],
            stage_in.at[slot, pl.ds(8 * half, 8)],
            in_sem.at[slot, half],
        )

    def proj_copy(job):
        slot = (job + 1) % 3
        return pltpu.make_async_copy(
            proj.at[pl.ds(16 * job, 16)], stage_in.at[slot], in_sem.at[slot, 0]
        )

    state_copy(0).start()
    barrier = pltpu.get_barrier_semaphore()
    for mask in ALL_MASKS:
        pl.semaphore_signal(
            barrier, inc=1, device_id={"dom": flip_bits(me, mask)}, device_id_type=MESH
        )
    mates = []
    for relation in range(1, 4):
        mate_pool = (pool + relation // 2) % 2
        mate_band = (band + relation % 2) % 2
        mates.append((mate_pool, mate_band))
        pl.semaphore_signal(
            barrier,
            inc=1,
            device_id={"pool": mate_pool, "band": mate_band},
            device_id_type=MESH,
        )

    for chunk in range(1, 6):
        state_copy(chunk).start()
    small = [
        pltpu.make_async_copy(source, held, small_sem.at[at])
        for at, (source, held) in enumerate(
            (
                (flips_in, flips),
                (numer_in, numer),
                (pot_in, pot),
                (ids_in, ids),
                (coupling_in, coupling),
                (occupation_in, occupation),
                (k_own_in, k_own),
                (k_low_in, k_low),
                (k_up_in, k_up),
            )
        )
    ]
    for copy in small:
        copy.start()

    def halo_copies(phase, chunk, wanted):
        turn = CH * phase + chunk
        source = cur if phase == 0 else nxt
        plan = (
            (send_y.at[chunk, 1 - odd_y], recv_y.at[turn, 0], 2),
            (send_y.at[chunk, odd_y], recv_y.at[turn, 1], 4),
            (send_x.at[chunk, 1 - odd_x], recv_x.at[turn, 0], 8),
            (send_x.at[chunk, odd_x], recv_x.at[turn, 1], 16),
            (source.at[chunk], recv_z.at[turn], 1),
        )
        return [
            pltpu.make_async_remote_copy(
                src_ref=src,
                dst_ref=dst,
                send_sem=send_sem.at[turn, at],
                recv_sem=recv_sem.at[turn, at],
                device_id={"dom": flip_bits(me, mask)},
                device_id_type=MESH,
            )
            for at, (src, dst, mask) in enumerate(plan)
            if at in wanted
        ]

    lane8 = lax.broadcasted_iota(jnp.int32, (1, 8, 128), 2)

    def enqueue(phase, chunk):
        source = cur if phase == 0 else nxt
        copies = halo_copies(phase, chunk, range(5))
        for face, first in ((0, 0), (1, CY - HALO)):
            value = jnp.concatenate(
                [source[chunk, pl.ds(x * CY + first, HALO)] for x in range(XL)], axis=0
            )
            tail = value[YROWS : YROWS + 3]
            for piece in range(15):
                send_y[chunk, face, 3 * piece : 3 * piece + 3] = jnp.where(
                    lane8 < USED, value[3 * piece : 3 * piece + 3], roll(tail, USED - 8 * piece)
                )
        copies[0].start()
        copies[1].start()
        copies[4].start()
        for face, first in ((0, 0), (1, 2 * CY)):
            parts = [
                roll(
                    source[chunk, pl.ds(first + XROWS * group, XROWS)],
                    CZ * group - (GROUPS - 1) * CZ * face,
                )
                for group in range(GROUPS)
            ]
            send_x[chunk, face] = jnp.where(
                lane8 < CZ, parts[0], jnp.where(lane8 < 2 * CZ, parts[1], parts[2])
            )
        copies[2].start()
        copies[3].start()

    def inner_part(phase, chunk):
        turn = CH * phase + chunk
        source, target = (cur, nxt) if phase == 0 else (nxt, cur)

        def z_part(half, carry):
            at = pl.ds(half * (ROWS // 2), ROWS // 2)
            left = jnp.concatenate(
                [
                    source[chunk, at].reshape(ROWS * 4, 128),
                    recv_z[turn, at].reshape(ROWS * 4, 128),
                ],
                axis=1,
            )
            high, rest = split(left)
            wide = jnp.dot(high, kz[...], preferred_element_type=F32)
            narrow = jnp.dot(rest, kz[:, :128], preferred_element_type=F32)
            total = (wide[:, :128] + wide[:, 128:] + narrow).reshape(ROWS // 2, 8, 128)
            if phase == 0:
                target[chunk, at] = total
            else:
                target[chunk, at] = total + total - target[chunk, at]
            return carry

        lax.fori_loop(0, 2, z_part, 0)

        for x in range(XL):
            ext_y[x, HALO : HALO + CY] = source[chunk, x * CY : x * CY + CY]

        for group in range(GROUPS):
            lower = recv_x[turn, 1 - odd_x] * low_x
            ext_x[XROWS * group : XROWS * group + XROWS] = jnp.where(
                lane8 < CZ,
                roll(lower, -CZ * group),
                roll(source[chunk, pl.ds(2 * CY + XROWS * group, XROWS)], CZ),
            )
            upper = recv_x[turn, odd_x] * up_x
            start = (HALO + XL) * CY + XROWS * group
            ext_x[start : start + XROWS] = jnp.where(
                lane8 >= 2 * CZ,
                roll(upper, CZ * (GROUPS - 1 - group)),
                roll(source[chunk, pl.ds(XROWS * group, XROWS)], -CZ),
            )
        ext_x[HALO * CY : (HALO + XL) * CY] = source[chunk]

        def rest_part(step, carry):
            x, half = step // 2, step % 2
            at = pl.ds(x * CY + half * 10, 10)
            column = ext_y[x, pl.ds(half * 10, 10 + 2 * HALO)]
            total = potential[at] * column[HALO : HALO + 10]
            for shift in range(1, HALO + 1):
                pair = column[HALO + shift : HALO + shift + 10] + column[HALO - shift : HALO - shift + 10]
                above = ext_x[pl.ds((x + HALO + shift) * CY + half * 10, 10)]
                below = ext_x[pl.ds((x + HALO - shift) * CY + half * 10, 10)]
                total = total + (SCALE * COEFFS[shift]) * (pair + (above + below))
            if phase == 0:
                target[chunk, at] = target[chunk, at] + total
            else:
                target[chunk, at] = target[chunk, at] + (total + total)
            return carry

        lax.fori_loop(0, 2 * XL, rest_part, 0)

    def y_halo_part(phase, chunk):
        turn = CH * phase + chunk
        target = nxt if phase == 0 else cur
        scale = SCALE * (phase + 1.0)
        for face, slot_of, sign in ((0, 1 - odd_y, low_y), (1, odd_y, up_y)):
            tail = jnp.zeros((3, 8, 128), F32)
            for piece in range(15):
                value = recv_y[turn, slot_of, 3 * piece : 3 * piece + 3]
                halo_y[face, 3 * piece : 3 * piece + 3] = value * sign
                moved = roll(value, 8 * piece - USED)
                tail = jnp.where((lane8 >= 8 * piece) & (lane8 < 8 * piece + 8), moved, tail)
            halo_y[face, YROWS : YROWS + 3] = tail * sign

        def column(x, carry):
            low = halo_y[0, pl.ds(HALO * x, HALO)]
            up = halo_y[1, pl.ds(HALO * x, HALO)]
            first, last = [], []
            for y in range(HALO):
                first.append(
                    sum(
                        (scale * COEFFS[shift]) * low[HALO + y - shift]
                        for shift in range(y + 1, HALO + 1)
                    )
                )
                last.append(
                    sum(
                        (scale * COEFFS[shift]) * up[y + shift - HALO]
                        for shift in range(HALO - y, HALO + 1)
                    )
                )
            at = pl.ds(x * CY, HALO)
            target[chunk, at] = target[chunk, at] + jnp.stack(first)
            at = pl.ds(x * CY + CY - HALO, HALO)
            target[chunk, at] = target[chunk, at] + jnp.stack(last)
            return carry

        lax.fori_loop(0, XL, column, 0, unroll=4)

    own_slot = core * 16 + me // 2

    def gather_copies(phase, stage):
        buffer = gather1 if phase == 0 else gather2
        if stage == 0:
            masks, block = Y_MASKS, buffer.at[own_slot]
        elif stage == 1:
            masks, block = X_MASKS, buffer.at[pl.ds(core * 16 + code_x * 4, 4)]
        else:
            masks, block = (1,), buffer.at[pl.ds(core * 16, 16)]
        return [
            pltpu.make_async_remote_copy(
                src_ref=block,
                dst_ref=block,
                send_sem=gsend_sem.at[phase, 3 * stage + at],
                recv_sem=grecv_sem.at[phase, 3 * stage + at],
                device_id={"dom": flip_bits(me, mask)},
                device_id_type=MESH,
            )
            for at, mask in enumerate(masks)
        ]

    def gather_start(phase, stage):
        for copy in gather_copies(phase, stage):
            copy.start()

    def gather_wait(phase, stage):
        for copy in gather_copies(phase, stage):
            copy.wait()

    lane32 = lanes_of(32)

    def coefficients(phase):
        source = cur if phase == 0 else nxt
        buffer = gather1 if phase == 0 else gather2

        def step(pair, total):
            left = jnp.concatenate(
                [source[:, 2 * pair + part].reshape(STATES, 128) for part in range(2)], axis=1
            )
            both = jnp.concatenate(split(left), axis=0)
            return total + lax.dot_general(
                both, pbox[pair], (((1,), (1,)), ((), ())), preferred_element_type=F32
            )

        total = lax.fori_loop(0, PAIRS, step, jnp.zeros((128, 128), F32), unroll=4)
        total = total + roll(total, 64)
        total = total[:STATES] + total[STATES:]
        buffer[own_slot, 0:32] = jnp.where(lane32 < 64, total[:32], total[32:])

    def nonlocal_rows(phase):
        buffer = gather1 if phase == 0 else gather2

        def step(slot, total):
            block = buffer[slot, 0:32]
            pieces = []
            for piece in split(block):
                wide = piece.astype(F32)
                pieces.append(jnp.where(lane32 < 64, wide, 0.0))
                pieces.append(jnp.where(lane32 < 64, 0.0, wide))
            left = jnp.concatenate(pieces, axis=0).astype(BF16)
            return total + lax.dot_general(
                left, same[slot], (((1,), (1,)), ((), ())), preferred_element_type=F32
            )

        total = lax.fori_loop(0, 32, step, jnp.zeros((128, 128), F32), unroll=4)
        weights = (total[:STATES] + total[STATES:]) * coupling_row
        weights = weights * ((phase + 1.0) / HALF_WIDTH)
        left = jnp.concatenate(split(weights), axis=1)

        def spread(pair, carry):
            right = jnp.concatenate([pbox[pair], pbox[pair]], axis=0)
            both = jnp.dot(left, right, preferred_element_type=F32)
            nonloc[:, 2 * pair] = both[:, :128].reshape(CH, 8, 128)
            nonloc[:, 2 * pair + 1] = both[:, 128:].reshape(CH, 8, 128)
            return carry

        lax.fori_loop(0, PAIRS, spread, 0, unroll=4)

    def bring_states(chunk):
        state_copy(chunk).wait()
        slot, half = (chunk // 2) % 3, chunk % 2

        def block(index, carry):
            def load(group, tile):
                start = pl.multiple_of(THIRD * group + 640 * index + 128 * tile, 128)
                return stage_in[slot, 8 * half : 8 * half + 8, pl.ds(start, 128)]

            def put(line, row):
                cur[chunk, LINES * index + line] = row

            rows_from_lines(load, 8, put)
            return carry

        lax.fori_loop(0, BLOCKS, block, 0, unroll=5)

    bring_states(0)
    pl.semaphore_wait(barrier, len(ALL_MASKS) + 3)
    enqueue(0, 0)
    bring_states(1)
    enqueue(0, 1)
    state_copy(6).start()
    state_copy(7).start()
    bring_states(2)
    enqueue(0, 2)
    bring_states(3)
    proj_copy(0).start()
    bring_states(4)
    bring_states(5)
    proj_copy(1).start()
    bring_states(6)
    bring_states(7)
    proj_copy(2).start()

    for copy in small:
        copy.wait()
    def sign_of(direction, at_edge):
        flip = flips[:, direction : direction + 1].astype(F32) * at_edge.astype(F32)
        return jnp.broadcast_to(1.0 - 2.0 * flip, (8, 128))

    low_x, up_x = sign_of(0, place_x == 0), sign_of(0, place_x == 3)
    low_y, up_y = sign_of(1, place_y == 0), sign_of(1, place_y == 3)
    low_z, up_z = sign_of(2, core == 0), sign_of(2, core == 1)

    own_numer = numer[...].astype(F32)
    count_note[0] = jnp.broadcast_to(own_numer, (1, 128))
    count_copy = pltpu.make_async_remote_copy(
        src_ref=count_note.at[0],
        dst_ref=count_note.at[1],
        send_sem=nsend_sem.at[3],
        recv_sem=nrecv_sem.at[3],
        device_id={"pool": (pool + 1) % 2, "band": band},
        device_id_type=MESH,
    )
    count_copy.start()
    def diagonal(size):
        return lax.broadcasted_iota(jnp.int32, (size, size), 0) == lax.broadcasted_iota(
            jnp.int32, (size, size), 1
        )

    id_row = ids[...].astype(F32)
    id_pair = jnp.concatenate([id_row, id_row], axis=1)
    id_column = jnp.sum(jnp.where(diagonal(128), id_pair, 0.0), axis=1, keepdims=True)
    gather1[own_slot, 32:40] = jnp.broadcast_to(id_pair, (8, 128))

    for job in range(4):
        proj_copy(job).wait()

        def proj_block(index, carry):
            held = []

            def load(group, tile):
                start = pl.multiple_of(THIRD * group + 640 * index + 128 * tile, 128)
                return stage_in[(job + 1) % 3, :, pl.ds(start, 128)]

            def put(line, row):
                held.append(row)
                if line % 2 == 1:
                    high, rest = split(jnp.concatenate(held[-2:], axis=1))
                    pair = (LINES // 2) * index + line // 2
                    pbox[pair, 16 * job : 16 * job + 16] = high
                    pbox[pair, SLOTS + 16 * job : SLOTS + 16 * job + 16] = rest

            rows_from_lines(load, 16, put)
            return carry

        lax.fori_loop(0, BLOCKS, proj_block, 0, unroll=5)
        if job == 0:
            proj_copy(3).start()

    coefficients(0)
    gather_start(0, 0)
    enqueue(0, 3)

    for x in range(XL):
        ext_y[x, 0:HALO] = jnp.zeros((HALO, 8, 128), F32)
        ext_y[x, HALO + CY :] = jnp.zeros((HALO, 8, 128), F32)
    kz[0:128] = k_own[...]
    kz[128:256] = (
        k_low[...].astype(F32) * low_z[0:1, 0:1] + k_up[...].astype(F32) * up_z[0:1, 0:1]
    ).astype(BF16)

    def potential_block(index, carry):
        def load(group, tile):
            start = pl.multiple_of(THIRD * group + 640 * index + 128 * tile, 128)
            return jnp.broadcast_to(pot[:, pl.ds(start, 128)], (8, 128))

        def put(line, row):
            potential[LINES * index + line] = (row - CENTER) / HALF_WIDTH + 3.0 * SCALE * COEFFS[0]

        rows_from_lines(load, 8, put)
        return carry

    lax.fori_loop(0, BLOCKS, potential_block, 0, unroll=5)

    all_ids = lax.broadcasted_iota(jnp.int32, (128, 512), 1).astype(F32)
    strength = jnp.sum(
        jnp.where(all_ids == id_column, coupling[...], 0.0), axis=1, keepdims=True
    )
    coupling_row = jnp.sum(jnp.where(diagonal(128), strength, 0.0), axis=0, keepdims=True)
    occ_column = jnp.sum(
        jnp.where(diagonal(STATES), occupation[...], 0.0), axis=1, keepdims=True
    )
    occ_rows[...] = jnp.broadcast_to(occ_column * own_numer, (STATES, 128)).reshape(CH, 8, 128)
    rho[...] = jnp.zeros((1, CELLS), F32)

    def wait_y(phase, chunk):
        for copy in halo_copies(phase, chunk, (0, 1)):
            copy.wait()

    def wait_rest(phase, chunk):
        for copy in halo_copies(phase, chunk, (2, 3, 4)):
            copy.wait()

    def phase_one(chunk, carry):
        wait_y(0, chunk)

        @pl.when(chunk == 2)
        def _():
            gather_wait(0, 0)
            gather_start(0, 1)

        @pl.when(chunk == 3)
        def _():
            gather_wait(0, 1)
            gather_start(0, 2)

        @pl.when((chunk >= 2) & (chunk < 6))
        def _():
            enqueue(0, chunk + 2)

        @pl.when(chunk >= 6)
        def _():
            enqueue(1, chunk - 6)

        y_halo_part(0, chunk)

        @pl.when(chunk == 4)
        def _():
            gather_wait(0, 2)

            def compare(slot, inner):
                same[slot] = jnp.where(id_column == gather1[slot, 32:33], 1.0, 0.0).astype(BF16)
                return inner

            lax.fori_loop(0, 32, compare, 0)
            nonlocal_rows(0)

        def finish(done, inner):
            nxt[done] = nxt[done] + nonloc[done]
            return inner

        low = jnp.where(chunk == 4, 0, chunk)
        high = jnp.where(chunk < 4, chunk, chunk + 1)
        lax.fori_loop(low, high, finish, 0)

        @pl.when(chunk < CH - 1)
        def _():
            wait_rest(0, chunk + 1)
            inner_part(0, chunk + 1)

        return carry

    wait_rest(0, 0)
    inner_part(0, 0)
    lax.fori_loop(0, CH, phase_one, 0)

    coefficients(1)
    gather_start(1, 0)

    def phase_two(chunk, carry):
        wait_y(1, chunk)

        @pl.when(chunk == 1)
        def _():
            gather_wait(1, 0)
            gather_start(1, 1)

        @pl.when(chunk == 2)
        def _():
            gather_wait(1, 1)
            gather_start(1, 2)

        @pl.when(chunk < 6)
        def _():
            enqueue(1, chunk + 2)

        y_halo_part(1, chunk)

        @pl.when(chunk == 3)
        def _():
            gather_wait(1, 2)
            nonlocal_rows(1)

        def finish(done, inner):
            weight = occ_rows[done]

            def block(index, deep):
                at = pl.ds(LINES * index, LINES)
                value = cur[done, at] + nonloc[done, at]
                def put(group, tile, found):
                    start = pl.multiple_of(THIRD * group + 640 * index + 128 * tile, 128)
                    out[pl.ds(pl.multiple_of(8 * done, 8), 8), pl.ds(start, 128)] = found
                    rho[:, pl.ds(start, 128)] = rho[:, pl.ds(start, 128)] + jnp.sum(
                        found * found * weight, axis=0, keepdims=True
                    )

                lines_from_rows([value[line] for line in range(LINES)], put)
                return deep

            lax.fori_loop(0, BLOCKS, block, 0, unroll=10)
            return inner

        low = jnp.where(chunk == 3, 0, chunk)
        high = jnp.where(chunk < 3, chunk, chunk + 1)
        lax.fori_loop(low, high, finish, 0)

        @pl.when(chunk < CH - 1)
        def _():
            wait_rest(1, chunk + 1)
            inner_part(1, chunk + 1)

        return carry

    wait_rest(1, 0)
    inner_part(1, 0)
    lax.fori_loop(0, CH, phase_two, 0)

    def quarter_of(mate_pool, mate_band):
        start = pl.multiple_of(128 * (75 * (2 * mate_pool + mate_band) // 2), 128)
        return pl.ds(start, PIECE)

    note_copies = [
        pltpu.make_async_remote_copy(
            src_ref=rho.at[:, quarter_of(mate_pool, mate_band)],
            dst_ref=got_notes.at[at],
            send_sem=nsend_sem.at[at],
            recv_sem=nrecv_sem.at[at],
            device_id={"pool": mate_pool, "band": mate_band},
            device_id_type=MESH,
        )
        for at, (mate_pool, mate_band) in enumerate(mates)
    ]
    for copy in note_copies[::-1]:
        copy.start()
    count_copy.wait()
    total_numer = count_note[0] + count_note[1]
    for copy in note_copies:
        copy.wait()
    total = rho[:, quarter_of(pool, band)] + got_notes[0] + got_notes[1] + got_notes[2]
    total = jnp.where(band == 1, total[:, 64:PIECE], total[:, : PIECE - 64])
    dens[...] = total / total_numer[:, 0:1]


def body(
    states_in, bloch_flip, kweight_num, local_pot, proj_values, proj_ids, coupling, occupation
):
    k_own, k_low, k_up = z_matrices()
    vmem = pl.BlockSpec(memory_space=pltpu.VMEM)
    hbm = pl.BlockSpec(memory_space=pl.ANY)
    dma = pltpu.SemaphoreType.DMA
    out, dens = pl.pallas_call(
        kernel,
        out_shape=(
            pltpu.VMEM((STATES, CELLS), F32),
            pltpu.VMEM((1, CELLS // 4), F32),
        ),
        in_specs=[hbm] * 11,
        out_specs=(vmem, vmem),
        scratch_shapes=[
            pltpu.VMEM((CH, ROWS, 8, 128), F32),
            pltpu.VMEM((CH, ROWS, 8, 128), F32),
            pltpu.VMEM((CH, ROWS, 8, 128), F32),
            pltpu.VMEM((PAIRS, 2 * SLOTS, 256), BF16),
            pltpu.VMEM((CH, 2, YROWS, 8, 128), F32),
            pltpu.VMEM((CH, 2, XROWS, 8, 128), F32),
            pltpu.VMEM((2 * CH, 2, YROWS, 8, 128), F32),
            pltpu.VMEM((2 * CH, 2, XROWS, 8, 128), F32),
            pltpu.VMEM((2 * CH, ROWS, 8, 128), F32),
            pltpu.VMEM(((XL + 2 * HALO) * CY, 8, 128), F32),
            pltpu.VMEM((XL, CY + 2 * HALO, 8, 128), F32),
            pltpu.VMEM((2, XL * HALO, 8, 128), F32),
            pltpu.VMEM((ROWS, 8, 128), F32),
            pltpu.VMEM((256, 256), BF16),
            pltpu.VMEM((32, 40, 128), F32),
            pltpu.VMEM((32, 32, 128), F32),
            pltpu.VMEM((32, 128, 128), BF16),
            pltpu.VMEM((CH, 8, 128), F32),
            pltpu.VMEM((1, CELLS), F32),
            pltpu.VMEM((2, 1, 128), F32),
            pltpu.VMEM((3, 1, PIECE), F32),
            pltpu.VMEM((3, 16, CELLS), F32),
            pltpu.VMEM((1, 3), jnp.int32),
            pltpu.VMEM((1, 1), jnp.int32),
            pltpu.VMEM((1, CELLS), F32),
            pltpu.VMEM((1, SLOTS), jnp.int32),
            pltpu.VMEM((1, 512), F32),
            pltpu.VMEM((1, STATES), F32),
            pltpu.VMEM((128, 256), BF16),
            pltpu.VMEM((128, 256), BF16),
            pltpu.VMEM((128, 256), BF16),
            dma((3, 2)),
            dma((9,)),
            dma((2 * CH, 5)),
            dma((2 * CH, 5)),
            dma((2, 9)),
            dma((2, 9)),
            dma((4,)),
            dma((4,)),
        ],
        compiler_params=pltpu.CompilerParams(
            collective_id=0, has_side_effects=True, vmem_limit_bytes=58 << 20
        ),
    )(
        states_in[0, 0],
        bloch_flip,
        kweight_num[None],
        local_pot,
        proj_values[0],
        proj_ids,
        coupling[None],
        occupation[None],
        k_own,
        k_low,
        k_up,
    )

    def move(held, held_dens, result, result_dens, sem):
        copies = [
            pltpu.make_async_copy(held.at[pl.ds(8 * at, 8)], result.at[pl.ds(8 * at, 8)], sem.at[at])
            for at in range(CH)
        ]
        copies.append(pltpu.make_async_copy(held_dens, result_dens, sem.at[CH]))
        for copy in copies:
            copy.start()
        for copy in copies:
            copy.wait()

    out, dens = pl.pallas_call(
        move,
        out_shape=(
            jax.ShapeDtypeStruct((STATES, CELLS), F32),
            jax.ShapeDtypeStruct((1, CELLS // 4), F32),
        ),
        in_specs=[vmem, vmem],
        out_specs=(hbm, hbm),
        scratch_shapes=[dma((CH + 1,))],
        compiler_params=pltpu.CompilerParams(vmem_limit_bytes=1 << 20),
    )(
        pltpu.with_memory_space_constraint(out, pltpu.VMEM),
        pltpu.with_memory_space_constraint(dens, pltpu.VMEM),
    )
    return out[None, None], dens


def solution(mesh):
    placed = (
        P("pool", "dom", "band", None),
        P("pool", None),
        P("pool"),
        P("dom", None),
        P("dom", None, None),
        P("dom", None),
        P(),
        P("band"),
    )
    return jax.shard_map(
        body,
        mesh=mesh,
        in_specs=placed,
        out_specs=(P("pool", "dom", "band", None), P("dom", ("pool", "band"))),
        check_vma=False,
    )
```

```python
import jax
import jax.numpy as jnp
import numpy as np
from jax import lax
from jax.experimental import pallas as pl
from jax.experimental.pallas import tpu as pltpu
from jax.sharding import PartitionSpec as P

MESH = pl.DeviceIdType.MESH
F32 = jnp.float32
BF16 = jnp.bfloat16

HALO = 6
CX = 24
CY = 20
CZ = 40
CELLS = CX * CY * CZ
COEFFS = (
    -5369.0 / 1800.0,
    12.0 / 7.0,
    -15.0 / 56.0,
    10.0 / 189.0,
    -1.0 / 112.0,
    2.0 / 1925.0,
    -1.0 / 16632.0,
)
CENTER = 14.0
HALF_WIDTH = 10.0
SCALE = -0.5 / HALF_WIDTH

GROUPS = 3
XL = CX // GROUPS
ROWS = XL * CY
USED = GROUPS * CZ
THIRD = CELLS // GROUPS
BLOCKS = 10
LINES = 16
STATES = 64
CH = 8
SLOTS = 64
PAIRS = ROWS // 2
YROWS = 45
XROWS = 40
PIECE = 4864

Y_MASKS = (2, 4, 6)
X_MASKS = (8, 16, 24)
ALL_MASKS = (1,) + Y_MASKS + X_MASKS


def z_matrices():
    own = np.zeros((128, 128), np.float64)
    low = np.zeros((128, 128), np.float64)
    up = np.zeros((128, 128), np.float64)
    for group in range(GROUPS):
        for z in range(CZ):
            for shift in range(1, HALO + 1):
                for source in (z + shift, z - shift):
                    target = own if 0 <= source < CZ else (low if source < 0 else up)
                    target[group * CZ + source % CZ, group * CZ + z] += SCALE * COEFFS[shift]
    pairs = []
    for matrix in (own, low, up):
        high = jnp.asarray(matrix, F32).astype(BF16)
        rest = (jnp.asarray(matrix, F32) - high.astype(F32)).astype(BF16)
        pairs.append(jnp.concatenate([high, rest], axis=1))
    return pairs


def flip_bits(me, mask):
    other = me
    for bit in (1, 2, 4, 8, 16):
        if mask & bit:
            other = other + bit * (1 - 2 * ((me // bit) % 2))
    return other


def lanes_of(rows):
    return lax.broadcasted_iota(jnp.int32, (rows, 128), 1)


def roll(value, shift):
    shift = shift % 128
    if shift == 0:
        return value
    return pltpu.roll(value, shift, value.ndim - 1)


def split(value):
    high = value.astype(BF16)
    return high, (value - high.astype(F32)).astype(BF16)


def rows_from_lines(load, count, put):
    lane = lanes_of(count)
    tiles = [[load(group, tile) for tile in range(5)] for group in range(GROUPS)]
    for line in range(LINES):
        tile, offset = divmod(CZ * line, 128)
        parts = []
        for group in range(GROUPS):
            value = tiles[group][tile]
            if offset + CZ > 128:
                value = jnp.where(lane >= offset, value, tiles[group][tile + 1])
            parts.append(roll(value, CZ * group - offset))
        row = jnp.where(lane < CZ, parts[0], jnp.where(lane < 2 * CZ, parts[1], parts[2]))
        put(line, jnp.where(lane < USED, row, 0.0))


def lines_from_rows(rows, put):
    lane = lanes_of(8)
    for group in range(GROUPS):
        for tile in range(5):
            first, offset = divmod(128 * tile, CZ)
            value = None
            for step in range(4):
                part = roll(rows[first + step], CZ * step - offset - CZ * group)
                value = part if step == 0 else jnp.where(lane < CZ * step - offset, value, part)
            put(group, tile, value)


def kernel(
    states,
    flips_in,
    numer_in,
    pot_in,
    proj,
    ids_in,
    coupling_in,
    occupation_in,
    k_own_in,
    k_low_in,
    k_up_in,
    out,
    dens,
    cur,
    nxt,
    nonloc,
    pbox,
    send_y,
    send_x,
    recv_y,
    recv_x,
    recv_z,
    ext_x,
    ext_y,
    halo_y,
    potential,
    kz,
    gather1,
    gather2,
    same,
    occ_rows,
    rho,
    count_note,
    got_notes,
    stage_in,
    flips,
    numer,
    pot,
    ids,
    coupling,
    occupation,
    k_own,
    k_low,
    k_up,
    in_sem,
    small_sem,
    send_sem,
    recv_sem,
    gsend_sem,
    grecv_sem,
    nsend_sem,
    nrecv_sem,
):
    me = lax.axis_index("dom")
    pool = lax.axis_index("pool")
    band = lax.axis_index("band")
    core = me % 2
    code_y = (me // 2) % 4
    code_x = me // 8

    def place_of(code):
        return code + (code // 2) * (1 - 2 * (code % 2))

    place_y = place_of(code_y)
    place_x = place_of(code_x)
    odd_y = place_y % 2
    odd_x = place_x % 2

    def state_copy(chunk):
        slot, half = (chunk // 2) % 3, chunk % 2
        return pltpu.make_async_copy(
            states.at[pl.ds(8 * chunk, 8)],
            stage_in.at[slot, pl.ds(8 * half, 8)],
            in_sem.at[slot, half],
        )

    def proj_copy(job):
        slot = (job + 1) % 3
        return pltpu.make_async_copy(
            proj.at[pl.ds(16 * job, 16)], stage_in.at[slot], in_sem.at[slot, 0]
        )

    state_copy(0).start()
    barrier = pltpu.get_barrier_semaphore()
    for mask in ALL_MASKS:
        pl.semaphore_signal(
            barrier, inc=1, device_id={"dom": flip_bits(me, mask)}, device_id_type=MESH
        )
    mates = []
    for relation in range(1, 4):
        mate_pool = (pool + relation // 2) % 2
        mate_band = (band + relation % 2) % 2
        mates.append((mate_pool, mate_band))
        pl.semaphore_signal(
            barrier,
            inc=1,
            device_id={"pool": mate_pool, "band": mate_band},
            device_id_type=MESH,
        )

    for chunk in range(1, 6):
        state_copy(chunk).start()
    small = [
        pltpu.make_async_copy(source, held, small_sem.at[at])
        for at, (source, held) in enumerate(
            (
                (flips_in, flips),
                (numer_in, numer),
                (pot_in, pot),
                (ids_in, ids),
                (coupling_in, coupling),
                (occupation_in, occupation),
                (k_own_in, k_own),
                (k_low_in, k_low),
                (k_up_in, k_up),
            )
        )
    ]
    for copy in small:
        copy.start()

    def halo_copies(phase, chunk, wanted):
        turn = CH * phase + chunk
        source = cur if phase == 0 else nxt
        plan = (
            (send_y.at[chunk, 1 - odd_y], recv_y.at[turn, 0], 2),
            (send_y.at[chunk, odd_y], recv_y.at[turn, 1], 4),
            (send_x.at[chunk, 1 - odd_x], recv_x.at[turn, 0], 8),
            (send_x.at[chunk, odd_x], recv_x.at[turn, 1], 16),
            (source.at[chunk], recv_z.at[turn], 1),
        )
        return [
            pltpu.make_async_remote_copy(
                src_ref=src,
                dst_ref=dst,
                send_sem=send_sem.at[turn, at],
                recv_sem=recv_sem.at[turn, at],
                device_id={"dom": flip_bits(me, mask)},
                device_id_type=MESH,
            )
            for at, (src, dst, mask) in enumerate(plan)
            if at in wanted
        ]

    lane8 = lax.broadcasted_iota(jnp.int32, (1, 8, 128), 2)

    def enqueue(phase, chunk):
        source = cur if phase == 0 else nxt
        copies = halo_copies(phase, chunk, range(5))
        for face, first in ((0, 0), (1, CY - HALO)):
            value = jnp.concatenate(
                [source[chunk, pl.ds(x * CY + first, HALO)] for x in range(XL)], axis=0
            )
            tail = value[YROWS : YROWS + 3]
            for piece in range(15):
                send_y[chunk, face, 3 * piece : 3 * piece + 3] = jnp.where(
                    lane8 < USED, value[3 * piece : 3 * piece + 3], roll(tail, USED - 8 * piece)
                )
        copies[0].start()
        copies[1].start()
        copies[4].start()
        for face, first in ((0, 0), (1, 2 * CY)):
            parts = [
                roll(
                    source[chunk, pl.ds(first + XROWS * group, XROWS)],
                    CZ * group - (GROUPS - 1) * CZ * face,
                )
                for group in range(GROUPS)
            ]
            send_x[chunk, face] = jnp.where(
                lane8 < CZ, parts[0], jnp.where(lane8 < 2 * CZ, parts[1], parts[2])
            )
        copies[2].start()
        copies[3].start()

    def inner_part(phase, chunk):
        turn = CH * phase + chunk
        source, target = (cur, nxt) if phase == 0 else (nxt, cur)

        def z_part(half, carry):
            at = pl.ds(half * (ROWS // 2), ROWS // 2)
            left = jnp.concatenate(
                [
                    source[chunk, at].reshape(ROWS * 4, 128),
                    recv_z[turn, at].reshape(ROWS * 4, 128),
                ],
                axis=1,
            )
            high, rest = split(left)
            wide = jnp.dot(high, kz[...], preferred_element_type=F32)
            narrow = jnp.dot(rest, kz[:, :128], preferred_element_type=F32)
            total = (wide[:, :128] + wide[:, 128:] + narrow).reshape(ROWS // 2, 8, 128)
            if phase == 0:
                target[chunk, at] = total
            else:
                target[chunk, at] = total + total - target[chunk, at]
            return carry

        lax.fori_loop(0, 2, z_part, 0)

        for x in range(XL):
            ext_y[x, HALO : HALO + CY] = source[chunk, x * CY : x * CY + CY]

        for group in range(GROUPS):
            lower = recv_x[turn, 1 - odd_x] * low_x
            ext_x[XROWS * group : XROWS * group + XROWS] = jnp.where(
                lane8 < CZ,
                roll(lower, -CZ * group),
                roll(source[chunk, pl.ds(2 * CY + XROWS * group, XROWS)], CZ),
            )
            upper = recv_x[turn, odd_x] * up_x
            start = (HALO + XL) * CY + XROWS * group
            ext_x[start : start + XROWS] = jnp.where(
                lane8 >= 2 * CZ,
                roll(upper, CZ * (GROUPS - 1 - group)),
                roll(source[chunk, pl.ds(XROWS * group, XROWS)], -CZ),
            )
        ext_x[HALO * CY : (HALO + XL) * CY] = source[chunk]

        def rest_part(step, carry):
            x, half = step // 2, step % 2
            at = pl.ds(x * CY + half * 10, 10)
            column = ext_y[x, pl.ds(half * 10, 10 + 2 * HALO)]
            total = potential[at] * column[HALO : HALO + 10]
            for shift in range(1, HALO + 1):
                pair = column[HALO + shift : HALO + shift + 10] + column[HALO - shift : HALO - shift + 10]
                above = ext_x[pl.ds((x + HALO + shift) * CY + half * 10, 10)]
                below = ext_x[pl.ds((x + HALO - shift) * CY + half * 10, 10)]
                total = total + (SCALE * COEFFS[shift]) * (pair + (above + below))
            if phase == 0:
                target[chunk, at] = target[chunk, at] + total
            else:
                target[chunk, at] = target[chunk, at] + (total + total)
            return carry

        lax.fori_loop(0, 2 * XL, rest_part, 0)

    def y_halo_part(phase, chunk):
        turn = CH * phase + chunk
        target = nxt if phase == 0 else cur
        scale = SCALE * (phase + 1.0)
        for face, slot_of, sign in ((0, 1 - odd_y, low_y), (1, odd_y, up_y)):
            tail = jnp.zeros((3, 8, 128), F32)
            for piece in range(15):
                value = recv_y[turn, slot_of, 3 * piece : 3 * piece + 3]
                halo_y[face, 3 * piece : 3 * piece + 3] = value * sign
                moved = roll(value, 8 * piece - USED)
                tail = jnp.where((lane8 >= 8 * piece) & (lane8 < 8 * piece + 8), moved, tail)
            halo_y[face, YROWS : YROWS + 3] = tail * sign

        def column(x, carry):
            low = halo_y[0, pl.ds(HALO * x, HALO)]
            up = halo_y[1, pl.ds(HALO * x, HALO)]
            first, last = [], []
            for y in range(HALO):
                first.append(
                    sum(
                        (scale * COEFFS[shift]) * low[HALO + y - shift]
                        for shift in range(y + 1, HALO + 1)
                    )
                )
                last.append(
                    sum(
                        (scale * COEFFS[shift]) * up[y + shift - HALO]
                        for shift in range(HALO - y, HALO + 1)
                    )
                )
            at = pl.ds(x * CY, HALO)
            target[chunk, at] = target[chunk, at] + jnp.stack(first)
            at = pl.ds(x * CY + CY - HALO, HALO)
            target[chunk, at] = target[chunk, at] + jnp.stack(last)
            return carry

        lax.fori_loop(0, XL, column, 0, unroll=4)

    own_slot = core * 16 + me // 2

    def gather_copies(phase, stage):
        buffer = gather1 if phase == 0 else gather2
        if stage == 0:
            masks, block = (2, 6), buffer.at[own_slot]
        elif stage == 1:
            masks, block = (6,), buffer.at[core * 16 + flip_bits(me, 2) // 2]
        elif stage == 2:
            masks, block = X_MASKS, buffer.at[pl.ds(core * 16 + code_x * 4, 4)]
        else:
            masks, block = (1,), buffer.at[pl.ds(core * 16, 16)]
        return [
            pltpu.make_async_remote_copy(
                src_ref=block,
                dst_ref=block,
                send_sem=gsend_sem.at[phase, 3 * stage + at],
                recv_sem=grecv_sem.at[phase, 3 * stage + at],
                device_id={"dom": flip_bits(me, mask)},
                device_id_type=MESH,
            )
            for at, mask in enumerate(masks)
        ]

    def gather_start(phase, stage):
        for copy in gather_copies(phase, stage):
            copy.start()

    def gather_wait(phase, stage):
        for copy in gather_copies(phase, stage):
            copy.wait()

    lane32 = lanes_of(32)

    def coefficients(phase):
        source = cur if phase == 0 else nxt
        buffer = gather1 if phase == 0 else gather2

        def step(pair, total):
            left = jnp.concatenate(
                [source[:, 2 * pair + part].reshape(STATES, 128) for part in range(2)], axis=1
            )
            both = jnp.concatenate(split(left), axis=0)
            return total + lax.dot_general(
                both, pbox[pair], (((1,), (1,)), ((), ())), preferred_element_type=F32
            )

        total = lax.fori_loop(0, PAIRS, step, jnp.zeros((128, 128), F32), unroll=4)
        total = total + roll(total, 64)
        total = total[:STATES] + total[STATES:]
        buffer[own_slot, 0:32] = jnp.where(lane32 < 64, total[:32], total[32:])

    def nonlocal_rows(phase):
        buffer = gather1 if phase == 0 else gather2

        def step(slot, total):
            block = buffer[slot, 0:32]
            pieces = []
            for piece in split(block):
                wide = piece.astype(F32)
                pieces.append(jnp.where(lane32 < 64, wide, 0.0))
                pieces.append(jnp.where(lane32 < 64, 0.0, wide))
            left = jnp.concatenate(pieces, axis=0).astype(BF16)
            return total + lax.dot_general(
                left, same[slot], (((1,), (1,)), ((), ())), preferred_element_type=F32
            )

        total = lax.fori_loop(0, 32, step, jnp.zeros((128, 128), F32), unroll=4)
        weights = (total[:STATES] + total[STATES:]) * coupling_row
        weights = weights * ((phase + 1.0) / HALF_WIDTH)
        left = jnp.concatenate(split(weights), axis=1)

        def spread(pair, carry):
            right = jnp.concatenate([pbox[pair], pbox[pair]], axis=0)
            both = jnp.dot(left, right, preferred_element_type=F32)
            nonloc[:, 2 * pair] = both[:, :128].reshape(CH, 8, 128)
            nonloc[:, 2 * pair + 1] = both[:, 128:].reshape(CH, 8, 128)
            return carry

        lax.fori_loop(0, PAIRS, spread, 0, unroll=4)

    def bring_states(chunk):
        state_copy(chunk).wait()
        slot, half = (chunk // 2) % 3, chunk % 2

        def block(index, carry):
            def load(group, tile):
                start = pl.multiple_of(THIRD * group + 640 * index + 128 * tile, 128)
                return stage_in[slot, 8 * half : 8 * half + 8, pl.ds(start, 128)]

            def put(line, row):
                cur[chunk, LINES * index + line] = row

            rows_from_lines(load, 8, put)
            return carry

        lax.fori_loop(0, BLOCKS, block, 0, unroll=5)

    bring_states(0)
    pl.semaphore_wait(barrier, len(ALL_MASKS) + 3)
    enqueue(0, 0)
    bring_states(1)
    enqueue(0, 1)
    state_copy(6).start()
    state_copy(7).start()
    bring_states(2)
    enqueue(0, 2)
    bring_states(3)
    proj_copy(0).start()
    bring_states(4)
    bring_states(5)
    proj_copy(1).start()
    bring_states(6)
    bring_states(7)
    proj_copy(2).start()

    for copy in small:
        copy.wait()
    def sign_of(direction, at_edge):
        flip = flips[:, direction : direction + 1].astype(F32) * at_edge.astype(F32)
        return jnp.broadcast_to(1.0 - 2.0 * flip, (8, 128))

    low_x, up_x = sign_of(0, place_x == 0), sign_of(0, place_x == 3)
    low_y, up_y = sign_of(1, place_y == 0), sign_of(1, place_y == 3)
    low_z, up_z = sign_of(2, core == 0), sign_of(2, core == 1)

    own_numer = numer[...].astype(F32)
    count_note[0] = jnp.broadcast_to(own_numer, (1, 128))
    count_copy = pltpu.make_async_remote_copy(
        src_ref=count_note.at[0],
        dst_ref=count_note.at[1],
        send_sem=nsend_sem.at[3],
        recv_sem=nrecv_sem.at[3],
        device_id={"pool": (pool + 1) % 2, "band": band},
        device_id_type=MESH,
    )
    count_copy.start()
    def diagonal(size):
        return lax.broadcasted_iota(jnp.int32, (size, size), 0) == lax.broadcasted_iota(
            jnp.int32, (size, size), 1
        )

    id_row = ids[...].astype(F32)
    id_pair = jnp.concatenate([id_row, id_row], axis=1)
    id_column = jnp.sum(jnp.where(diagonal(128), id_pair, 0.0), axis=1, keepdims=True)
    gather1[own_slot, 32:40] = jnp.broadcast_to(id_pair, (8, 128))

    for job in range(4):
        proj_copy(job).wait()

        def proj_block(index, carry):
            held = []

            def load(group, tile):
                start = pl.multiple_of(THIRD * group + 640 * index + 128 * tile, 128)
                return stage_in[(job + 1) % 3, :, pl.ds(start, 128)]

            def put(line, row):
                held.append(row)
                if line % 2 == 1:
                    high, rest = split(jnp.concatenate(held[-2:], axis=1))
                    pair = (LINES // 2) * index + line // 2
                    pbox[pair, 16 * job : 16 * job + 16] = high
                    pbox[pair, SLOTS + 16 * job : SLOTS + 16 * job + 16] = rest

            rows_from_lines(load, 16, put)
            return carry

        lax.fori_loop(0, BLOCKS, proj_block, 0, unroll=5)
        if job == 0:
            proj_copy(3).start()

    coefficients(0)
    gather_start(0, 0)
    enqueue(0, 3)

    for x in range(XL):
        ext_y[x, 0:HALO] = jnp.zeros((HALO, 8, 128), F32)
        ext_y[x, HALO + CY :] = jnp.zeros((HALO, 8, 128), F32)
    kz[0:128] = k_own[...]
    kz[128:256] = (
        k_low[...].astype(F32) * low_z[0:1, 0:1] + k_up[...].astype(F32) * up_z[0:1, 0:1]
    ).astype(BF16)

    def potential_block(index, carry):
        def load(group, tile):
            start = pl.multiple_of(THIRD * group + 640 * index + 128 * tile, 128)
            return jnp.broadcast_to(pot[:, pl.ds(start, 128)], (8, 128))

        def put(line, row):
            potential[LINES * index + line] = (row - CENTER) / HALF_WIDTH + 3.0 * SCALE * COEFFS[0]

        rows_from_lines(load, 8, put)
        return carry

    lax.fori_loop(0, BLOCKS, potential_block, 0, unroll=5)

    all_ids = lax.broadcasted_iota(jnp.int32, (128, 512), 1).astype(F32)
    strength = jnp.sum(
        jnp.where(all_ids == id_column, coupling[...], 0.0), axis=1, keepdims=True
    )
    coupling_row = jnp.sum(jnp.where(diagonal(128), strength, 0.0), axis=0, keepdims=True)
    occ_column = jnp.sum(
        jnp.where(diagonal(STATES), occupation[...], 0.0), axis=1, keepdims=True
    )
    occ_rows[...] = jnp.broadcast_to(occ_column * own_numer, (STATES, 128)).reshape(CH, 8, 128)
    rho[...] = jnp.zeros((1, CELLS), F32)

    def wait_y(phase, chunk):
        for copy in halo_copies(phase, chunk, (0, 1)):
            copy.wait()

    def wait_rest(phase, chunk):
        for copy in halo_copies(phase, chunk, (2, 3, 4)):
            copy.wait()

    def phase_one(chunk, carry):
        wait_y(0, chunk)

        @pl.when(chunk == 2)
        def _():
            gather_wait(0, 0)
            gather_start(0, 1)

        @pl.when(chunk == 3)
        def _():
            gather_wait(0, 1)
            gather_start(0, 2)

        @pl.when(chunk == 4)
        def _():
            gather_wait(0, 2)
            gather_start(0, 3)

        @pl.when((chunk >= 2) & (chunk < 6))
        def _():
            enqueue(0, chunk + 2)

        @pl.when(chunk >= 6)
        def _():
            enqueue(1, chunk - 6)

        y_halo_part(0, chunk)

        @pl.when(chunk == 5)
        def _():
            gather_wait(0, 3)

            def compare(slot, inner):
                same[slot] = jnp.where(id_column == gather1[slot, 32:33], 1.0, 0.0).astype(BF16)
                return inner

            lax.fori_loop(0, 32, compare, 0)
            nonlocal_rows(0)

        def finish(done, inner):
            nxt[done] = nxt[done] + nonloc[done]
            return inner

        low = jnp.where(chunk == 5, 0, chunk)
        high = jnp.where(chunk < 5, chunk, chunk + 1)
        lax.fori_loop(low, high, finish, 0)

        @pl.when(chunk < CH - 1)
        def _():
            wait_rest(0, chunk + 1)
            inner_part(0, chunk + 1)

        return carry

    wait_rest(0, 0)
    inner_part(0, 0)
    lax.fori_loop(0, CH, phase_one, 0)

    coefficients(1)
    gather_start(1, 0)

    def phase_two(chunk, carry):
        wait_y(1, chunk)

        @pl.when(chunk == 1)
        def _():
            gather_wait(1, 0)
            gather_start(1, 1)

        @pl.when(chunk == 2)
        def _():
            gather_wait(1, 1)
            gather_start(1, 2)

        @pl.when(chunk == 3)
        def _():
            gather_wait(1, 2)
            gather_start(1, 3)

        @pl.when(chunk < 6)
        def _():
            enqueue(1, chunk + 2)

        y_halo_part(1, chunk)

        @pl.when(chunk == 4)
        def _():
            gather_wait(1, 3)
            nonlocal_rows(1)

        def finish(done, inner):
            weight = occ_rows[done]

            def block(index, deep):
                at = pl.ds(LINES * index, LINES)
                value = cur[done, at] + nonloc[done, at]
                def put(group, tile, found):
                    start = pl.multiple_of(THIRD * group + 640 * index + 128 * tile, 128)
                    out[pl.ds(pl.multiple_of(8 * done, 8), 8), pl.ds(start, 128)] = found
                    rho[:, pl.ds(start, 128)] = rho[:, pl.ds(start, 128)] + jnp.sum(
                        found * found * weight, axis=0, keepdims=True
                    )

                lines_from_rows([value[line] for line in range(LINES)], put)
                return deep

            lax.fori_loop(0, BLOCKS, block, 0, unroll=10)
            return inner

        low = jnp.where(chunk == 4, 0, chunk)
        high = jnp.where(chunk < 4, chunk, chunk + 1)
        lax.fori_loop(low, high, finish, 0)

        @pl.when(chunk < CH - 1)
        def _():
            wait_rest(1, chunk + 1)
            inner_part(1, chunk + 1)

        return carry

    wait_rest(1, 0)
    inner_part(1, 0)
    lax.fori_loop(0, CH, phase_two, 0)

    def quarter_of(mate_pool, mate_band):
        start = pl.multiple_of(128 * (75 * (2 * mate_pool + mate_band) // 2), 128)
        return pl.ds(start, PIECE)

    note_copies = [
        pltpu.make_async_remote_copy(
            src_ref=rho.at[:, quarter_of(mate_pool, mate_band)],
            dst_ref=got_notes.at[at],
            send_sem=nsend_sem.at[at],
            recv_sem=nrecv_sem.at[at],
            device_id={"pool": mate_pool, "band": mate_band},
            device_id_type=MESH,
        )
        for at, (mate_pool, mate_band) in enumerate(mates)
    ]
    for at in (1, 2, 0):
        note_copies[at].start()
    count_copy.wait()
    total_numer = count_note[0] + count_note[1]
    for copy in note_copies:
        copy.wait()
    total = rho[:, quarter_of(pool, band)] + got_notes[0] + got_notes[1] + got_notes[2]
    total = jnp.where(band == 1, total[:, 64:PIECE], total[:, : PIECE - 64])
    dens[...] = total / total_numer[:, 0:1]


def body(
    states_in, bloch_flip, kweight_num, local_pot, proj_values, proj_ids, coupling, occupation
):
    k_own, k_low, k_up = z_matrices()
    vmem = pl.BlockSpec(memory_space=pltpu.VMEM)
    hbm = pl.BlockSpec(memory_space=pl.ANY)
    dma = pltpu.SemaphoreType.DMA
    out, dens = pl.pallas_call(
        kernel,
        out_shape=(
            pltpu.VMEM((STATES, CELLS), F32),
            pltpu.VMEM((1, CELLS // 4), F32),
        ),
        in_specs=[hbm] * 11,
        out_specs=(vmem, vmem),
        scratch_shapes=[
            pltpu.VMEM((CH, ROWS, 8, 128), F32),
            pltpu.VMEM((CH, ROWS, 8, 128), F32),
            pltpu.VMEM((CH, ROWS, 8, 128), F32),
            pltpu.VMEM((PAIRS, 2 * SLOTS, 256), BF16),
            pltpu.VMEM((CH, 2, YROWS, 8, 128), F32),
            pltpu.VMEM((CH, 2, XROWS, 8, 128), F32),
            pltpu.VMEM((2 * CH, 2, YROWS, 8, 128), F32),
            pltpu.VMEM((2 * CH, 2, XROWS, 8, 128), F32),
            pltpu.VMEM((2 * CH, ROWS, 8, 128), F32),
            pltpu.VMEM(((XL + 2 * HALO) * CY, 8, 128), F32),
            pltpu.VMEM((XL, CY + 2 * HALO, 8, 128), F32),
            pltpu.VMEM((2, XL * HALO, 8, 128), F32),
            pltpu.VMEM((ROWS, 8, 128), F32),
            pltpu.VMEM((256, 256), BF16),
            pltpu.VMEM((32, 40, 128), F32),
            pltpu.VMEM((32, 32, 128), F32),
            pltpu.VMEM((32, 128, 128), BF16),
            pltpu.VMEM((CH, 8, 128), F32),
            pltpu.VMEM((1, CELLS), F32),
            pltpu.VMEM((2, 1, 128), F32),
            pltpu.VMEM((3, 1, PIECE), F32),
            pltpu.VMEM((3, 16, CELLS), F32),
            pltpu.VMEM((1, 3), jnp.int32),
            pltpu.VMEM((1, 1), jnp.int32),
            pltpu.VMEM((1, CELLS), F32),
            pltpu.VMEM((1, SLOTS), jnp.int32),
            pltpu.VMEM((1, 512), F32),
            pltpu.VMEM((1, STATES), F32),
            pltpu.VMEM((128, 256), BF16),
            pltpu.VMEM((128, 256), BF16),
            pltpu.VMEM((128, 256), BF16),
            dma((3, 2)),
            dma((9,)),
            dma((2 * CH, 5)),
            dma((2 * CH, 5)),
            dma((2, 12)),
            dma((2, 12)),
            dma((4,)),
            dma((4,)),
        ],
        compiler_params=pltpu.CompilerParams(
            collective_id=0, has_side_effects=True, vmem_limit_bytes=58 << 20
        ),
    )(
        states_in[0, 0],
        bloch_flip,
        kweight_num[None],
        local_pot,
        proj_values[0],
        proj_ids,
        coupling[None],
        occupation[None],
        k_own,
        k_low,
        k_up,
    )

    def move(held, held_dens, result, result_dens, sem):
        copies = [
            pltpu.make_async_copy(held.at[pl.ds(8 * at, 8)], result.at[pl.ds(8 * at, 8)], sem.at[at])
            for at in range(CH)
        ]
        copies.append(pltpu.make_async_copy(held_dens, result_dens, sem.at[CH]))
        for copy in copies:
            copy.start()
        for copy in copies:
            copy.wait()

    out, dens = pl.pallas_call(
        move,
        out_shape=(
            jax.ShapeDtypeStruct((STATES, CELLS), F32),
            jax.ShapeDtypeStruct((1, CELLS // 4), F32),
        ),
        in_specs=[vmem, vmem],
        out_specs=(hbm, hbm),
        scratch_shapes=[dma((CH + 1,))],
        compiler_params=pltpu.CompilerParams(vmem_limit_bytes=1 << 20),
    )(
        pltpu.with_memory_space_constraint(out, pltpu.VMEM),
        pltpu.with_memory_space_constraint(dens, pltpu.VMEM),
    )
    return out[None, None], dens


def solution(mesh):
    placed = (
        P("pool", "dom", "band", None),
        P("pool", None),
        P("pool"),
        P("dom", None),
        P("dom", None, None),
        P("dom", None),
        P(),
        P("band"),
    )
    return jax.shard_map(
        body,
        mesh=mesh,
        in_specs=placed,
        out_specs=(P("pool", "dom", "band", None), P("dom", ("pool", "band"))),
        check_vma=False,
    )
```

```python
import jax
import jax.numpy as jnp
import numpy as np
from jax import lax
from jax.experimental import pallas as pl
from jax.experimental.pallas import tpu as pltpu
from jax.sharding import PartitionSpec as P

MESH = pl.DeviceIdType.MESH
F32 = jnp.float32
BF16 = jnp.bfloat16

HALO = 6
CX = 24
CY = 20
CZ = 40
CELLS = CX * CY * CZ
COEFFS = (
    -5369.0 / 1800.0,
    12.0 / 7.0,
    -15.0 / 56.0,
    10.0 / 189.0,
    -1.0 / 112.0,
    2.0 / 1925.0,
    -1.0 / 16632.0,
)
CENTER = 14.0
HALF_WIDTH = 10.0
SCALE = -0.5 / HALF_WIDTH

GROUPS = 3
XL = CX // GROUPS
ROWS = XL * CY
USED = GROUPS * CZ
THIRD = CELLS // GROUPS
BLOCKS = 10
LINES = 16
STATES = 64
CH = 8
SLOTS = 64
PAIRS = ROWS // 2
YROWS = 45
XROWS = 40
PIECE = 4864

Y_MASKS = (2, 4, 6)
X_MASKS = (8, 16, 24)
ALL_MASKS = (1,) + Y_MASKS + X_MASKS


def z_matrices():
    own = np.zeros((128, 128), np.float64)
    low = np.zeros((128, 128), np.float64)
    up = np.zeros((128, 128), np.float64)
    for group in range(GROUPS):
        for z in range(CZ):
            for shift in range(1, HALO + 1):
                for source in (z + shift, z - shift):
                    target = own if 0 <= source < CZ else (low if source < 0 else up)
                    target[group * CZ + source % CZ, group * CZ + z] += SCALE * COEFFS[shift]
    pairs = []
    for matrix in (own, low, up):
        high = jnp.asarray(matrix, F32).astype(BF16)
        rest = (jnp.asarray(matrix, F32) - high.astype(F32)).astype(BF16)
        pairs.append(jnp.concatenate([high, rest], axis=1))
    return pairs


def flip_bits(me, mask):
    other = me
    for bit in (1, 2, 4, 8, 16):
        if mask & bit:
            other = other + bit * (1 - 2 * ((me // bit) % 2))
    return other


def lanes_of(rows):
    return lax.broadcasted_iota(jnp.int32, (rows, 128), 1)


def roll(value, shift):
    shift = shift % 128
    if shift == 0:
        return value
    return pltpu.roll(value, shift, value.ndim - 1)


def split(value):
    high = value.astype(BF16)
    return high, (value - high.astype(F32)).astype(BF16)


def rows_from_lines(load, count, put):
    lane = lanes_of(count)
    tiles = [[load(group, tile) for tile in range(5)] for group in range(GROUPS)]
    for line in range(LINES):
        tile, offset = divmod(CZ * line, 128)
        parts = []
        for group in range(GROUPS):
            value = tiles[group][tile]
            if offset + CZ > 128:
                value = jnp.where(lane >= offset, value, tiles[group][tile + 1])
            parts.append(roll(value, CZ * group - offset))
        row = jnp.where(lane < CZ, parts[0], jnp.where(lane < 2 * CZ, parts[1], parts[2]))
        put(line, jnp.where(lane < USED, row, 0.0))


def lines_from_rows(rows, put):
    lane = lanes_of(8)
    for group in range(GROUPS):
        for tile in range(5):
            first, offset = divmod(128 * tile, CZ)
            value = None
            for step in range(4):
                part = roll(rows[first + step], CZ * step - offset - CZ * group)
                value = part if step == 0 else jnp.where(lane < CZ * step - offset, value, part)
            put(group, tile, value)


def kernel(
    states,
    flips_in,
    numer_in,
    pot_in,
    proj,
    ids_in,
    coupling_in,
    occupation_in,
    k_own_in,
    k_low_in,
    k_up_in,
    out,
    dens,
    cur,
    nxt,
    nonloc,
    pbox,
    send_y,
    send_x,
    recv_y,
    recv_x,
    recv_z,
    ext_x,
    ext_y,
    halo_y,
    potential,
    kz,
    gather1,
    gather2,
    same,
    occ_rows,
    rho,
    count_note,
    got_notes,
    stage_in,
    flips,
    numer,
    pot,
    ids,
    coupling,
    occupation,
    k_own,
    k_low,
    k_up,
    in_sem,
    small_sem,
    send_sem,
    recv_sem,
    gsend_sem,
    grecv_sem,
    nsend_sem,
    nrecv_sem,
):
    me = lax.axis_index("dom")
    pool = lax.axis_index("pool")
    band = lax.axis_index("band")
    core = me % 2
    code_y = (me // 2) % 4
    code_x = me // 8

    def place_of(code):
        return code + (code // 2) * (1 - 2 * (code % 2))

    place_y = place_of(code_y)
    place_x = place_of(code_x)
    odd_y = place_y % 2
    odd_x = place_x % 2

    def state_copy(chunk):
        slot, half = (chunk // 2) % 3, chunk % 2
        return pltpu.make_async_copy(
            states.at[pl.ds(8 * chunk, 8)],
            stage_in.at[slot, pl.ds(8 * half, 8)],
            in_sem.at[slot, half],
        )

    def proj_copy(job):
        slot = (job + 1) % 3
        return pltpu.make_async_copy(
            proj.at[pl.ds(16 * job, 16)], stage_in.at[slot], in_sem.at[slot, 0]
        )

    state_copy(0).start()
    barrier = pltpu.get_barrier_semaphore()
    for mask in ALL_MASKS:
        pl.semaphore_signal(
            barrier, inc=1, device_id={"dom": flip_bits(me, mask)}, device_id_type=MESH
        )
    mates = []
    for relation in range(1, 4):
        mate_pool = (pool + relation // 2) % 2
        mate_band = (band + relation % 2) % 2
        mates.append((mate_pool, mate_band))
        pl.semaphore_signal(
            barrier,
            inc=1,
            device_id={"pool": mate_pool, "band": mate_band},
            device_id_type=MESH,
        )

    for chunk in range(1, 6):
        state_copy(chunk).start()
    small = [
        pltpu.make_async_copy(source, held, small_sem.at[at])
        for at, (source, held) in enumerate(
            (
                (flips_in, flips),
                (numer_in, numer),
                (pot_in, pot),
                (ids_in, ids),
                (coupling_in, coupling),
                (occupation_in, occupation),
                (k_own_in, k_own),
                (k_low_in, k_low),
                (k_up_in, k_up),
            )
        )
    ]
    for copy in small:
        copy.start()

    def halo_copies(phase, chunk, wanted):
        turn = CH * phase + chunk
        source = cur if phase == 0 else nxt
        plan = (
            (send_y.at[chunk, 1 - odd_y], recv_y.at[turn, 0], 2),
            (send_y.at[chunk, odd_y], recv_y.at[turn, 1], 4),
            (send_x.at[chunk, 1 - odd_x], recv_x.at[turn, 0], 8),
            (send_x.at[chunk, odd_x], recv_x.at[turn, 1], 16),
            (source.at[chunk], recv_z.at[turn], 1),
        )
        return [
            pltpu.make_async_remote_copy(
                src_ref=src,
                dst_ref=dst,
                send_sem=send_sem.at[turn, at],
                recv_sem=recv_sem.at[turn, at],
                device_id={"dom": flip_bits(me, mask)},
                device_id_type=MESH,
            )
            for at, (src, dst, mask) in enumerate(plan)
            if at in wanted
        ]

    lane8 = lax.broadcasted_iota(jnp.int32, (1, 8, 128), 2)

    def enqueue(phase, chunk):
        source = cur if phase == 0 else nxt
        copies = halo_copies(phase, chunk, range(5))
        for face, first in ((0, 0), (1, CY - HALO)):
            value = jnp.concatenate(
                [source[chunk, pl.ds(x * CY + first, HALO)] for x in range(XL)], axis=0
            )
            tail = value[YROWS : YROWS + 3]
            for piece in range(15):
                send_y[chunk, face, 3 * piece : 3 * piece + 3] = jnp.where(
                    lane8 < USED, value[3 * piece : 3 * piece + 3], roll(tail, USED - 8 * piece)
                )
        copies[1].start()
        copies[0].start()
        copies[4].start()
        for face, first in ((0, 0), (1, 2 * CY)):
            parts = [
                roll(
                    source[chunk, pl.ds(first + XROWS * group, XROWS)],
                    CZ * group - (GROUPS - 1) * CZ * face,
                )
                for group in range(GROUPS)
            ]
            send_x[chunk, face] = jnp.where(
                lane8 < CZ, parts[0], jnp.where(lane8 < 2 * CZ, parts[1], parts[2])
            )
        copies[3].start()
        copies[2].start()

    def inner_part(phase, chunk):
        turn = CH * phase + chunk
        source, target = (cur, nxt) if phase == 0 else (nxt, cur)

        def z_part(half, carry):
            at = pl.ds(half * (ROWS // 2), ROWS // 2)
            left = jnp.concatenate(
                [
                    source[chunk, at].reshape(ROWS * 4, 128),
                    recv_z[turn, at].reshape(ROWS * 4, 128),
                ],
                axis=1,
            )
            high, rest = split(left)
            wide = jnp.dot(high, kz[...], preferred_element_type=F32)
            narrow = jnp.dot(rest, kz[:, :128], preferred_element_type=F32)
            total = (wide[:, :128] + wide[:, 128:] + narrow).reshape(ROWS // 2, 8, 128)
            if phase == 0:
                target[chunk, at] = total
            else:
                target[chunk, at] = total + total - target[chunk, at]
            return carry

        lax.fori_loop(0, 2, z_part, 0)

        for x in range(XL):
            ext_y[x, HALO : HALO + CY] = source[chunk, x * CY : x * CY + CY]

        for group in range(GROUPS):
            lower = recv_x[turn, 1 - odd_x] * low_x
            ext_x[XROWS * group : XROWS * group + XROWS] = jnp.where(
                lane8 < CZ,
                roll(lower, -CZ * group),
                roll(source[chunk, pl.ds(2 * CY + XROWS * group, XROWS)], CZ),
            )
            upper = recv_x[turn, odd_x] * up_x
            start = (HALO + XL) * CY + XROWS * group
            ext_x[start : start + XROWS] = jnp.where(
                lane8 >= 2 * CZ,
                roll(upper, CZ * (GROUPS - 1 - group)),
                roll(source[chunk, pl.ds(XROWS * group, XROWS)], -CZ),
            )
        ext_x[HALO * CY : (HALO + XL) * CY] = source[chunk]

        def rest_part(step, carry):
            x, half = step // 2, step % 2
            at = pl.ds(x * CY + half * 10, 10)
            column = ext_y[x, pl.ds(half * 10, 10 + 2 * HALO)]
            total = potential[at] * column[HALO : HALO + 10]
            for shift in range(1, HALO + 1):
                pair = column[HALO + shift : HALO + shift + 10] + column[HALO - shift : HALO - shift + 10]
                above = ext_x[pl.ds((x + HALO + shift) * CY + half * 10, 10)]
                below = ext_x[pl.ds((x + HALO - shift) * CY + half * 10, 10)]
                total = total + (SCALE * COEFFS[shift]) * (pair + (above + below))
            if phase == 0:
                target[chunk, at] = target[chunk, at] + total
            else:
                target[chunk, at] = target[chunk, at] + (total + total)
            return carry

        lax.fori_loop(0, 2 * XL, rest_part, 0)

    def y_halo_part(phase, chunk):
        turn = CH * phase + chunk
        target = nxt if phase == 0 else cur
        scale = SCALE * (phase + 1.0)
        for face, slot_of, sign in ((0, 1 - odd_y, low_y), (1, odd_y, up_y)):
            tail = jnp.zeros((3, 8, 128), F32)
            for piece in range(15):
                value = recv_y[turn, slot_of, 3 * piece : 3 * piece + 3]
                halo_y[face, 3 * piece : 3 * piece + 3] = value * sign
                moved = roll(value, 8 * piece - USED)
                tail = jnp.where((lane8 >= 8 * piece) & (lane8 < 8 * piece + 8), moved, tail)
            halo_y[face, YROWS : YROWS + 3] = tail * sign

        def column(x, carry):
            low = halo_y[0, pl.ds(HALO * x, HALO)]
            up = halo_y[1, pl.ds(HALO * x, HALO)]
            first, last = [], []
            for y in range(HALO):
                first.append(
                    sum(
                        (scale * COEFFS[shift]) * low[HALO + y - shift]
                        for shift in range(y + 1, HALO + 1)
                    )
                )
                last.append(
                    sum(
                        (scale * COEFFS[shift]) * up[y + shift - HALO]
                        for shift in range(HALO - y, HALO + 1)
                    )
                )
            at = pl.ds(x * CY, HALO)
            target[chunk, at] = target[chunk, at] + jnp.stack(first)
            at = pl.ds(x * CY + CY - HALO, HALO)
            target[chunk, at] = target[chunk, at] + jnp.stack(last)
            return carry

        lax.fori_loop(0, XL, column, 0, unroll=4)

    own_slot = core * 16 + me // 2

    def gather_copies(phase, stage):
        buffer = gather1 if phase == 0 else gather2
        if stage == 0:
            masks, block = (2, 6), buffer.at[own_slot]
        elif stage == 1:
            masks, block = (6,), buffer.at[core * 16 + flip_bits(me, 2) // 2]
        elif stage == 2:
            masks, block = X_MASKS, buffer.at[pl.ds(core * 16 + code_x * 4, 4)]
        else:
            masks, block = (1,), buffer.at[pl.ds(core * 16, 16)]
        return [
            pltpu.make_async_remote_copy(
                src_ref=block,
                dst_ref=block,
                send_sem=gsend_sem.at[phase, 3 * stage + at],
                recv_sem=grecv_sem.at[phase, 3 * stage + at],
                device_id={"dom": flip_bits(me, mask)},
                device_id_type=MESH,
            )
            for at, mask in enumerate(masks)
        ]

    def gather_start(phase, stage):
        for copy in gather_copies(phase, stage):
            copy.start()

    def gather_wait(phase, stage):
        for copy in gather_copies(phase, stage):
            copy.wait()

    lane32 = lanes_of(32)

    def coefficients(phase):
        source = cur if phase == 0 else nxt
        buffer = gather1 if phase == 0 else gather2

        def step(pair, total):
            left = jnp.concatenate(
                [source[:, 2 * pair + part].reshape(STATES, 128) for part in range(2)], axis=1
            )
            both = jnp.concatenate(split(left), axis=0)
            return total + lax.dot_general(
                both, pbox[pair], (((1,), (1,)), ((), ())), preferred_element_type=F32
            )

        total = lax.fori_loop(0, PAIRS, step, jnp.zeros((128, 128), F32), unroll=4)
        total = total + roll(total, 64)
        total = total[:STATES] + total[STATES:]
        buffer[own_slot, 0:32] = jnp.where(lane32 < 64, total[:32], total[32:])

    def nonlocal_rows(phase):
        buffer = gather1 if phase == 0 else gather2

        def step(slot, total):
            block = buffer[slot, 0:32]
            pieces = []
            for piece in split(block):
                wide = piece.astype(F32)
                pieces.append(jnp.where(lane32 < 64, wide, 0.0))
                pieces.append(jnp.where(lane32 < 64, 0.0, wide))
            left = jnp.concatenate(pieces, axis=0).astype(BF16)
            return total + lax.dot_general(
                left, same[slot], (((1,), (1,)), ((), ())), preferred_element_type=F32
            )

        total = lax.fori_loop(0, 32, step, jnp.zeros((128, 128), F32), unroll=4)
        weights = (total[:STATES] + total[STATES:]) * coupling_row
        weights = weights * ((phase + 1.0) / HALF_WIDTH)
        left = jnp.concatenate(split(weights), axis=1)

        def spread(pair, carry):
            right = jnp.concatenate([pbox[pair], pbox[pair]], axis=0)
            both = jnp.dot(left, right, preferred_element_type=F32)
            nonloc[:, 2 * pair] = both[:, :128].reshape(CH, 8, 128)
            nonloc[:, 2 * pair + 1] = both[:, 128:].reshape(CH, 8, 128)
            return carry

        lax.fori_loop(0, PAIRS, spread, 0, unroll=4)

    def bring_states(chunk):
        state_copy(chunk).wait()
        slot, half = (chunk // 2) % 3, chunk % 2

        def block(index, carry):
            def load(group, tile):
                start = pl.multiple_of(THIRD * group + 640 * index + 128 * tile, 128)
                return stage_in[slot, 8 * half : 8 * half + 8, pl.ds(start, 128)]

            def put(line, row):
                cur[chunk, LINES * index + line] = row

            rows_from_lines(load, 8, put)
            return carry

        lax.fori_loop(0, BLOCKS, block, 0, unroll=5)

    bring_states(0)
    pl.semaphore_wait(barrier, len(ALL_MASKS) + 3)
    enqueue(0, 0)
    bring_states(1)
    enqueue(0, 1)
    state_copy(6).start()
    state_copy(7).start()
    bring_states(2)
    enqueue(0, 2)
    bring_states(3)
    proj_copy(0).start()
    bring_states(4)
    bring_states(5)
    proj_copy(1).start()
    bring_states(6)
    bring_states(7)
    proj_copy(2).start()

    for copy in small:
        copy.wait()
    def sign_of(direction, at_edge):
        flip = flips[:, direction : direction + 1].astype(F32) * at_edge.astype(F32)
        return jnp.broadcast_to(1.0 - 2.0 * flip, (8, 128))

    low_x, up_x = sign_of(0, place_x == 0), sign_of(0, place_x == 3)
    low_y, up_y = sign_of(1, place_y == 0), sign_of(1, place_y == 3)
    low_z, up_z = sign_of(2, core == 0), sign_of(2, core == 1)

    own_numer = numer[...].astype(F32)
    count_note[0] = jnp.broadcast_to(own_numer, (1, 128))
    count_copy = pltpu.make_async_remote_copy(
        src_ref=count_note.at[0],
        dst_ref=count_note.at[1],
        send_sem=nsend_sem.at[3],
        recv_sem=nrecv_sem.at[3],
        device_id={"pool": (pool + 1) % 2, "band": band},
        device_id_type=MESH,
    )
    count_copy.start()
    def diagonal(size):
        return lax.broadcasted_iota(jnp.int32, (size, size), 0) == lax.broadcasted_iota(
            jnp.int32, (size, size), 1
        )

    id_row = ids[...].astype(F32)
    id_pair = jnp.concatenate([id_row, id_row], axis=1)
    id_column = jnp.sum(jnp.where(diagonal(128), id_pair, 0.0), axis=1, keepdims=True)
    gather1[own_slot, 32:40] = jnp.broadcast_to(id_pair, (8, 128))

    for job in range(4):
        proj_copy(job).wait()

        def proj_block(index, carry):
            held = []

            def load(group, tile):
                start = pl.multiple_of(THIRD * group + 640 * index + 128 * tile, 128)
                return stage_in[(job + 1) % 3, :, pl.ds(start, 128)]

            def put(line, row):
                held.append(row)
                if line % 2 == 1:
                    high, rest = split(jnp.concatenate(held[-2:], axis=1))
                    pair = (LINES // 2) * index + line // 2
                    pbox[pair, 16 * job : 16 * job + 16] = high
                    pbox[pair, SLOTS + 16 * job : SLOTS + 16 * job + 16] = rest

            rows_from_lines(load, 16, put)
            return carry

        lax.fori_loop(0, BLOCKS, proj_block, 0, unroll=5)
        if job == 0:
            proj_copy(3).start()

    coefficients(0)
    gather_start(0, 0)
    enqueue(0, 3)

    for x in range(XL):
        ext_y[x, 0:HALO] = jnp.zeros((HALO, 8, 128), F32)
        ext_y[x, HALO + CY :] = jnp.zeros((HALO, 8, 128), F32)
    kz[0:128] = k_own[...]
    kz[128:256] = (
        k_low[...].astype(F32) * low_z[0:1, 0:1] + k_up[...].astype(F32) * up_z[0:1, 0:1]
    ).astype(BF16)

    def potential_block(index, carry):
        def load(group, tile):
            start = pl.multiple_of(THIRD * group + 640 * index + 128 * tile, 128)
            return jnp.broadcast_to(pot[:, pl.ds(start, 128)], (8, 128))

        def put(line, row):
            potential[LINES * index + line] = (row - CENTER) / HALF_WIDTH + 3.0 * SCALE * COEFFS[0]

        rows_from_lines(load, 8, put)
        return carry

    lax.fori_loop(0, BLOCKS, potential_block, 0, unroll=5)

    all_ids = lax.broadcasted_iota(jnp.int32, (128, 512), 1).astype(F32)
    strength = jnp.sum(
        jnp.where(all_ids == id_column, coupling[...], 0.0), axis=1, keepdims=True
    )
    coupling_row = jnp.sum(jnp.where(diagonal(128), strength, 0.0), axis=0, keepdims=True)
    occ_column = jnp.sum(
        jnp.where(diagonal(STATES), occupation[...], 0.0), axis=1, keepdims=True
    )
    occ_rows[...] = jnp.broadcast_to(occ_column * own_numer, (STATES, 128)).reshape(CH, 8, 128)
    rho[...] = jnp.zeros((1, CELLS), F32)

    def wait_y(phase, chunk):
        for copy in halo_copies(phase, chunk, (0, 1)):
            copy.wait()

    def wait_rest(phase, chunk):
        for copy in halo_copies(phase, chunk, (2, 3, 4)):
            copy.wait()

    def phase_one(chunk, carry):
        wait_y(0, chunk)

        @pl.when(chunk == 2)
        def _():
            gather_wait(0, 0)
            gather_start(0, 1)

        @pl.when(chunk == 3)
        def _():
            gather_wait(0, 1)
            gather_start(0, 2)

        @pl.when(chunk == 4)
        def _():
            gather_wait(0, 2)
            gather_start(0, 3)

        @pl.when((chunk >= 2) & (chunk < 6))
        def _():
            enqueue(0, chunk + 2)

        @pl.when(chunk >= 6)
        def _():
            enqueue(1, chunk - 6)

        y_halo_part(0, chunk)

        @pl.when(chunk == 5)
        def _():
            gather_wait(0, 3)

            def compare(slot, inner):
                same[slot] = jnp.where(id_column == gather1[slot, 32:33], 1.0, 0.0).astype(BF16)
                return inner

            lax.fori_loop(0, 32, compare, 0)
            nonlocal_rows(0)

        def finish(done, inner):
            nxt[done] = nxt[done] + nonloc[done]
            return inner

        low = jnp.where(chunk == 5, 0, chunk)
        high = jnp.where(chunk < 5, chunk, chunk + 1)
        lax.fori_loop(low, high, finish, 0)

        @pl.when(chunk < CH - 1)
        def _():
            wait_rest(0, chunk + 1)
            inner_part(0, chunk + 1)

        return carry

    wait_rest(0, 0)
    inner_part(0, 0)
    lax.fori_loop(0, CH, phase_one, 0)

    coefficients(1)
    gather_start(1, 0)

    def phase_two(chunk, carry):
        wait_y(1, chunk)

        @pl.when(chunk == 1)
        def _():
            gather_wait(1, 0)
            gather_start(1, 1)

        @pl.when(chunk == 2)
        def _():
            gather_wait(1, 1)
            gather_start(1, 2)

        @pl.when(chunk == 3)
        def _():
            gather_wait(1, 2)
            gather_start(1, 3)

        @pl.when(chunk < 6)
        def _():
            enqueue(1, chunk + 2)

        y_halo_part(1, chunk)

        @pl.when(chunk == 4)
        def _():
            gather_wait(1, 3)
            nonlocal_rows(1)

        def finish(done, inner):
            weight = occ_rows[done]

            def block(index, deep):
                at = pl.ds(LINES * index, LINES)
                value = cur[done, at] + nonloc[done, at]
                def put(group, tile, found):
                    start = pl.multiple_of(THIRD * group + 640 * index + 128 * tile, 128)
                    out[pl.ds(pl.multiple_of(8 * done, 8), 8), pl.ds(start, 128)] = found
                    rho[:, pl.ds(start, 128)] = rho[:, pl.ds(start, 128)] + jnp.sum(
                        found * found * weight, axis=0, keepdims=True
                    )

                lines_from_rows([value[line] for line in range(LINES)], put)
                return deep

            lax.fori_loop(0, BLOCKS, block, 0, unroll=10)
            return inner

        low = jnp.where(chunk == 4, 0, chunk)
        high = jnp.where(chunk < 4, chunk, chunk + 1)
        lax.fori_loop(low, high, finish, 0)

        @pl.when(chunk < CH - 1)
        def _():
            wait_rest(1, chunk + 1)
            inner_part(1, chunk + 1)

        return carry

    wait_rest(1, 0)
    inner_part(1, 0)
    lax.fori_loop(0, CH, phase_two, 0)

    def quarter_of(mate_pool, mate_band):
        start = pl.multiple_of(128 * (75 * (2 * mate_pool + mate_band) // 2), 128)
        return pl.ds(start, PIECE)

    note_copies = [
        pltpu.make_async_remote_copy(
            src_ref=rho.at[:, quarter_of(mate_pool, mate_band)],
            dst_ref=got_notes.at[at],
            send_sem=nsend_sem.at[at],
            recv_sem=nrecv_sem.at[at],
            device_id={"pool": mate_pool, "band": mate_band},
            device_id_type=MESH,
        )
        for at, (mate_pool, mate_band) in enumerate(mates)
    ]
    for at in (1, 2, 0):
        note_copies[at].start()
    count_copy.wait()
    total_numer = count_note[0] + count_note[1]
    for copy in note_copies:
        copy.wait()
    total = rho[:, quarter_of(pool, band)] + got_notes[0] + got_notes[1] + got_notes[2]
    total = jnp.where(band == 1, total[:, 64:PIECE], total[:, : PIECE - 64])
    dens[...] = total / total_numer[:, 0:1]


def body(
    states_in, bloch_flip, kweight_num, local_pot, proj_values, proj_ids, coupling, occupation
):
    k_own, k_low, k_up = z_matrices()
    vmem = pl.BlockSpec(memory_space=pltpu.VMEM)
    hbm = pl.BlockSpec(memory_space=pl.ANY)
    dma = pltpu.SemaphoreType.DMA
    out, dens = pl.pallas_call(
        kernel,
        out_shape=(
            pltpu.VMEM((STATES, CELLS), F32),
            pltpu.VMEM((1, CELLS // 4), F32),
        ),
        in_specs=[hbm] * 11,
        out_specs=(vmem, vmem),
        scratch_shapes=[
            pltpu.VMEM((CH, ROWS, 8, 128), F32),
            pltpu.VMEM((CH, ROWS, 8, 128), F32),
            pltpu.VMEM((CH, ROWS, 8, 128), F32),
            pltpu.VMEM((PAIRS, 2 * SLOTS, 256), BF16),
            pltpu.VMEM((CH, 2, YROWS, 8, 128), F32),
            pltpu.VMEM((CH, 2, XROWS, 8, 128), F32),
            pltpu.VMEM((2 * CH, 2, YROWS, 8, 128), F32),
            pltpu.VMEM((2 * CH, 2, XROWS, 8, 128), F32),
            pltpu.VMEM((2 * CH, ROWS, 8, 128), F32),
            pltpu.VMEM(((XL + 2 * HALO) * CY, 8, 128), F32),
            pltpu.VMEM((XL, CY + 2 * HALO, 8, 128), F32),
            pltpu.VMEM((2, XL * HALO, 8, 128), F32),
            pltpu.VMEM((ROWS, 8, 128), F32),
            pltpu.VMEM((256, 256), BF16),
            pltpu.VMEM((32, 40, 128), F32),
            pltpu.VMEM((32, 32, 128), F32),
            pltpu.VMEM((32, 128, 128), BF16),
            pltpu.VMEM((CH, 8, 128), F32),
            pltpu.VMEM((1, CELLS), F32),
            pltpu.VMEM((2, 1, 128), F32),
            pltpu.VMEM((3, 1, PIECE), F32),
            pltpu.VMEM((3, 16, CELLS), F32),
            pltpu.VMEM((1, 3), jnp.int32),
            pltpu.VMEM((1, 1), jnp.int32),
            pltpu.VMEM((1, CELLS), F32),
            pltpu.VMEM((1, SLOTS), jnp.int32),
            pltpu.VMEM((1, 512), F32),
            pltpu.VMEM((1, STATES), F32),
            pltpu.VMEM((128, 256), BF16),
            pltpu.VMEM((128, 256), BF16),
            pltpu.VMEM((128, 256), BF16),
            dma((3, 2)),
            dma((9,)),
            dma((2 * CH, 5)),
            dma((2 * CH, 5)),
            dma((2, 12)),
            dma((2, 12)),
            dma((4,)),
            dma((4,)),
        ],
        compiler_params=pltpu.CompilerParams(
            collective_id=0, has_side_effects=True, vmem_limit_bytes=58 << 20
        ),
    )(
        states_in[0, 0],
        bloch_flip,
        kweight_num[None],
        local_pot,
        proj_values[0],
        proj_ids,
        coupling[None],
        occupation[None],
        k_own,
        k_low,
        k_up,
    )

    def move(held, held_dens, result, result_dens, sem):
        copies = [
            pltpu.make_async_copy(held.at[pl.ds(8 * at, 8)], result.at[pl.ds(8 * at, 8)], sem.at[at])
            for at in range(CH)
        ]
        copies.append(pltpu.make_async_copy(held_dens, result_dens, sem.at[CH]))
        for copy in copies:
            copy.start()
        for copy in copies:
            copy.wait()

    out, dens = pl.pallas_call(
        move,
        out_shape=(
            jax.ShapeDtypeStruct((STATES, CELLS), F32),
            jax.ShapeDtypeStruct((1, CELLS // 4), F32),
        ),
        in_specs=[vmem, vmem],
        out_specs=(hbm, hbm),
        scratch_shapes=[dma((CH + 1,))],
        compiler_params=pltpu.CompilerParams(vmem_limit_bytes=1 << 20),
    )(
        pltpu.with_memory_space_constraint(out, pltpu.VMEM),
        pltpu.with_memory_space_constraint(dens, pltpu.VMEM),
    )
    return out[None, None], dens


def solution(mesh):
    placed = (
        P("pool", "dom", "band", None),
        P("pool", None),
        P("pool"),
        P("dom", None),
        P("dom", None, None),
        P("dom", None),
        P(),
        P("band"),
    )
    return jax.shard_map(
        body,
        mesh=mesh,
        in_specs=placed,
        out_specs=(P("pool", "dom", "band", None), P("dom", ("pool", "band"))),
        check_vma=False,
    )
```
